256 devices in a mesh: section: 16 (over x, z_hi), expert: 16 (over z_lo, y, core).
Axes of the slice: x: 4, y: 4, z: 8 (z_hi: 4, z_lo: 2; z = z_hi * 2 + z_lo), core: 2. Of those that a mesh axis runs over, the one named last changes fastest.
Arguments:
- entering: bfloat16 [2, 2, 512, 3584], P(None, None, 'expert'), may hold values from -6 to 6
- norm_gain: float32 [16, 3584], P('section'), may hold values from 0.5 to 1.5
- w_gate: bfloat16 [16, 3584, 8192], P('section', None, 'expert'), may hold values from -0.09375 to 0.09375
- w_up: bfloat16 [16, 3584, 8192], P('section', None, 'expert'), may hold values from -0.09375 to 0.09375
- w_down: bfloat16 [16, 8192, 3584], P('section', 'expert'), may hold values from -0.1875 to 0.1875
- route_ids: int32 [2, 2, 16, 512, 8], P(None, None, 'section', 'expert'), may hold values from 0 to 255, as said below
- route_scores: float32 [2, 2, 16, 512, 8], P(None, None, 'section', 'expert'), may hold values from 0.05 to 1
Outputs:
- leaving: bfloat16 [2, 2, 512, 3584], P(None, None, 'expert', 'section')
The draws below stay inside these ranges and needn't reach their ends.
Inputs may be any that keep to these rules, and one draw needn't show every extreme that they name: `route_ids`: A token's 8 ids are distinct. In every block of 32 tokens (one direction, micro-batch and layer), at most 2 tokens name any one expert below 8, and in every such block exactly 2 tokens name one of them.
All inputs are finite; a program needn't handle non-finite values.
Results may differ from the reference program's by a relative error of at most 0.0072.
Values may be sent and summed in bfloat16 or wider, within the bound.
A program may use at most 64 MiB of HBM per device.

```python
import math
import jax
import jax.numpy as jnp
from jax import lax

D = 3584
EXP_HID = 1024
EXPERTS = 256
TOPK = 8
GROUP = 2
CAP = 2
MICRO = 2
TOK_DEV = 32
LAYERS = 16
EXP_WIN = 8
TOKENS = 512
N_EXPERT = 16


def draw_route_ids(key, part):
    blocks = 2 * MICRO * LAYERS * (TOKENS // TOK_DEV)
    keys = jax.random.split(jax.random.fold_in(key, 7), 5)
    counts = jax.random.randint(keys[0], (blocks, EXP_WIN), 0, CAP + 1)
    forced = jax.random.randint(keys[1], (blocks, 1), 0, EXP_WIN)
    counts = jnp.where(jnp.arange(EXP_WIN)[None, :] == forced, CAP, counts)
    noise = jax.random.randint(keys[2], (blocks, EXP_WIN, TOK_DEV), 0, 65536) * TOK_DEV + jnp.arange(TOK_DEV)
    order = jnp.argsort(noise, axis=-1, stable=True)
    ranks = jnp.argsort(order, axis=-1, stable=True)
    member = ranks < counts[:, :, None]
    others = EXPERTS - EXP_WIN
    scores = jax.random.randint(keys[3], (blocks * TOK_DEV, others), 0, 65536) * others + jnp.arange(others)
    picks = jnp.argsort(scores, axis=-1, stable=True)[:, :TOPK] + EXP_WIN
    rotate = jax.random.randint(keys[4], (blocks * TOK_DEV, 1), 0, TOPK)
    member_rows = jnp.transpose(member, (0, 2, 1)).reshape(blocks * TOK_DEV, EXP_WIN)
    places = jnp.arange(TOPK)[None, :]
    chosen = picks
    for expert in range(EXP_WIN):
        marked = (places == (rotate + expert) % TOPK) & member_rows[:, expert:expert + 1]
        chosen = jnp.where(marked, expert, chosen)
    return chosen.reshape(2, MICRO, LAYERS, TOKENS, TOPK).astype(jnp.int32)


def block_levels(own_key, extent, cuts, smallest, high):
    loudness = 1.0
    for position, blocks in cuts:
        steps = jax.random.uniform(jax.random.fold_in(jax.random.fold_in(own_key, 6), position), (blocks,), jnp.float32, smallest / len(cuts), high / len(cuts))
        loudness = loudness * jnp.repeat(jnp.exp(steps), extent[position] // blocks).reshape((-1,) + (1,) * (len(extent) - 1 - position))
    return loudness


def normal_values(key, dims, scale, limit, pieces=(), kind=jnp.bfloat16):
    level = block_levels(key, dims, pieces, -0.22, 0.18) if pieces else 1.0
    drawn = jax.random.normal(key, dims, jnp.float32) * scale * level
    return jnp.minimum(jnp.maximum(drawn, -limit), limit).astype(kind)


def setup_inputs(seed: int = 0) -> dict:
    key_of = jax.random.split(jax.random.key(seed), 8)
    entering = normal_values(key_of[0], (2, MICRO, TOKENS, D), 1.0, 6.0, ((2, 16),))
    norm_gain = jnp.clip(1.0 + 0.1 * jax.random.normal(key_of[1], (LAYERS, D), jnp.float32), 0.5, 1.5)
    w_gate = normal_values(key_of[2], (LAYERS, D, EXP_WIN * EXP_HID), D ** -0.5, 0.09375, ((0, 16), (2, 16)))
    w_up = normal_values(key_of[3], (LAYERS, D, EXP_WIN * EXP_HID), D ** -0.5, 0.09375, ((0, 16), (2, 16)))
    w_down = normal_values(key_of[4], (LAYERS, EXP_WIN * EXP_HID, D), EXP_HID ** -0.5, 0.1875, ((0, 16), (1, 16)))
    route_ids = draw_route_ids(jax.random.fold_in(key_of[7], 71), 0)
    route_scores = jnp.clip(jnp.exp(math.log(1.0) - 2.9957323 * jax.random.uniform(key_of[6], (2, MICRO, LAYERS, TOKENS, TOPK), jnp.float32) ** block_levels(key_of[6], (2, MICRO, LAYERS, TOKENS, TOPK), ((2, 16), (3, 16)), -0.2, 0.2)), 0.05, 1.0)
    return dict(entering=entering, norm_gain=norm_gain, w_gate=w_gate, w_up=w_up, w_down=w_down, route_ids=route_ids, route_scores=route_scores)


norm_eps = 1e-06
route_scale = 2.5

def slot_tables(ids, weights):
    window = N_EXPERT // GROUP
    hit = (ids[:, :, :, None] == jnp.arange(window, dtype=jnp.int32)).astype(jnp.float32)
    count = lax.optimization_barrier(jnp.sum(hit, axis=2))
    share = lax.optimization_barrier(jnp.sum(weights[:, :, :, None] * hit, axis=2))
    before = jnp.cumsum(count, axis=1) - count
    slots = jnp.arange(CAP, dtype=jnp.float32)
    place = jnp.transpose(count, (0, 2, 1))[:, :, None, :] * (jnp.transpose(before, (0, 2, 1))[:, :, None, :] == slots[None, None, :, None]).astype(jnp.float32)
    comb = place * jnp.transpose(share, (0, 2, 1))[:, :, None, :]
    return (place, comb)

def layer(x, gain, wg, wu, wd, ids, scores):
    window = N_EXPERT // GROUP
    hid = EXP_HID // GROUP
    blocks = N_EXPERT
    xf = x.astype(jnp.float32)
    h = (xf * lax.rsqrt(lax.optimization_barrier(jnp.mean(xf * xf, axis=-1, keepdims=True)) + norm_eps) * gain).astype(jnp.bfloat16)
    weights = route_scale * scores / lax.optimization_barrier(jnp.sum(scores, axis=-1, keepdims=True))
    hb = h.reshape(blocks, TOK_DEV, D)
    place, comb = slot_tables(ids.reshape(blocks, TOK_DEV, TOPK), weights.reshape(blocks, TOK_DEV, TOPK))
    rows = jnp.einsum('bect,btd->becd', place, hb.astype(jnp.float32)).astype(jnp.bfloat16)
    outs = []
    for e in range(window):
        flat = rows[:, e].reshape(blocks * CAP, D)
        total = jnp.zeros((blocks * CAP, D), jnp.float32)
        for j in range(GROUP):
            lo = (e * GROUP + j) * hid
            gate = jnp.dot(flat, wg[:, lo:lo + hid], preferred_element_type=jnp.float32)
            up = jnp.dot(flat, wu[:, lo:lo + hid], preferred_element_type=jnp.float32)
            act = (jax.nn.silu(gate) * up).astype(jnp.bfloat16)
            part = jnp.dot(act, wd[lo:lo + hid, :], preferred_element_type=jnp.float32).astype(jnp.bfloat16)
            total = total + part.astype(jnp.float32)
        outs.append(total.reshape(blocks, CAP, D))
    expert_out = jnp.stack(outs, axis=1)
    added = jnp.einsum('bect,becd->btd', comb, expert_out, precision=lax.Precision.HIGHEST)
    return (xf + added.reshape(TOKENS, D)).astype(jnp.bfloat16)

def run(x, norm_gain, w_gate, w_up, w_down, ids, scores, backward):

    def one(carry, items):
        gain, wg, wu, wd, idl, scl = items
        return (layer(carry, gain, wg, wu, wd, idl, scl), None)
    final, unused = lax.scan(one, x, (norm_gain, w_gate, w_up, w_down, ids, scores), reverse=backward)
    return final

def reference(entering, norm_gain, w_gate, w_up, w_down, route_ids, route_scores):
    results = []
    for direction in range(2):
        row = []
        for micro in range(MICRO):
            row.append(run(entering[direction, micro], norm_gain, w_gate, w_up, w_down, route_ids[direction, micro], route_scores[direction, micro], direction == 1))
        results.append(jnp.stack(row))
    return jnp.stack(results)
```

```python
import jax
import jax.numpy as jnp
from jax import lax
from jax.experimental import pallas as pl
from jax.experimental.pallas import tpu as pltpu
from jax.sharding import PartitionSpec as P

MESH = pl.DeviceIdType.MESH
BF16, F32 = jnp.bfloat16, jnp.float32

GROUP = 2
CAP = 2
FLOWS = 4
WIDE = 256

norm_eps = 1e-06
route_scale = 2.5


def home_of(flow, sec):
    y = lax.rem(sec // 4 + sec + flow, 4)
    return (flow // 2) * 8 + y * 2 + lax.rem(flow, 2)


def kernel(
    xin, gain, tab, wg_h, wu_h, wd_h, out,
    wg, wu, wd, ein, eout, part, act, hx, hrows, hparts, fin,
    rowtok, rowwt, coltok, chi, clo, place,
    w_sem, init_send, init_recv, ein_sem, eout_sem, rows_sem, parts_sem, fin_send, fin_recv,
):
    sections = lax.axis_size("section")
    spread = lax.axis_size("expert")
    window = spread // GROUP
    sec, exp = lax.axis_index("section"), lax.axis_index("expert")
    tokens = xin.shape[1]
    width = wg_h.shape[0]
    chunk = width // sections
    hid = wg_h.shape[1]
    last = sections - 1
    half = spread // 2

    weights = [
        pltpu.make_async_copy(src, dst, w_sem.at[k])
        for k, (src, dst) in enumerate(((wg_h, wg), (wu_h, wu), (wd_h, wd)))
    ]
    for copy in weights:
        copy.start()

    flow = jnp.int32(-1)
    for f in range(FLOWS):
        flow = jnp.where(home_of(f, sec) == exp, f, flow)
    is_home = flow >= 0
    flow = jnp.maximum(flow, 0)
    way, micro = flow // 2, lax.rem(flow, 2)

    for f in range(FLOWS):
        home = home_of(f, sec)

        @pl.when(home == exp)
        def _():
            pltpu.make_async_copy(xin.at[f], hx.at[exp], init_recv).start()

        @pl.when(home != exp)
        def _():
            pltpu.make_async_remote_copy(
                src_ref=xin.at[f], dst_ref=hx.at[exp], send_sem=init_send.at[f], recv_sem=init_recv,
                device_id=(sec, home), device_id_type=MESH,
            ).start()

    eout[...] = jnp.zeros_like(eout)

    slots = half * CAP * window
    lane = lax.broadcasted_iota(jnp.int32, (1, slots), 1)
    lane_block = lax.rem(lane // CAP, half)

    @pl.when(is_home)
    def _():
        source = lax.broadcasted_iota(jnp.int32, (tab.shape[1], slots), 0)
        column = (lane // (half * CAP)) * CAP + lax.rem(lane, CAP)
        rows = lax.broadcasted_iota(jnp.int32, (tab.shape[0], slots), 0)
        own = lax.rem(rows, half) == lane_block
        picked = []
        for kind in range(2):
            pick = (source == (flow * 2 + kind) * (window * CAP) + column).astype(F32)
            spread_out = jnp.dot(
                tab[...], pick, precision=lax.Precision.HIGHEST, preferred_element_type=F32
            )
            kept = jnp.where(own, spread_out, 0.0).reshape(sections * 2, half, slots)
            picked.append(jnp.sum(kept, axis=1))
        tok = picked[0]
        tok = jnp.where(tok < -0.5, -1.0, tok + (lane_block * tokens).astype(F32))
        rowtok[...] = tok
        rowwt[...] = picked[1]
        coltok[...] = tok.T

    def home_phase(i):
        layer = jnp.where(way == 0, i, last - i)
        before = jnp.where(way == 0, i - 1, last - i + 1)
        count = half * tokens
        for g in range(2):

            @pl.when(i > 0)
            def _():
                row = before * 2 + g
                wide = lax.broadcasted_iota(jnp.int32, (count, slots), 0).astype(F32)
                comb = jnp.where(wide == rowtok[pl.ds(row, 1), :], rowwt[pl.ds(row, 1), :], 0.0)
                high = comb.astype(BF16)
                low = (comb - high.astype(F32)).astype(BF16)
                chi[g] = jnp.concatenate([high, high], axis=1)
                clo[g] = jnp.concatenate([low, low], axis=1)

            @pl.when(i <= last)
            def _():
                col = coltok[...]
                at = lax.broadcasted_iota(jnp.int32, col.shape, 1) == layer * 2 + g
                own = jnp.sum(jnp.where(at, col, 0.0), axis=1, keepdims=True)
                wide = lax.broadcasted_iota(jnp.int32, (slots, count), 1).astype(F32)
                place[g] = (wide == own).astype(BF16)

        @pl.when(i == 0)
        def _():
            pltpu.make_async_copy(hx, hx, init_recv).wait()

        @pl.when(i > 0)
        def _():
            step = i - 1
            pltpu.make_async_copy(hparts.at[step], hparts.at[step], parts_sem.at[step]).wait()
            for g in range(2):
                got = hparts[step, :, g * half * CAP : (g + 1) * half * CAP, :]
                got = got.reshape(2 * slots, WIDE)
                added = jnp.dot(chi[g], got, preferred_element_type=F32)
                added += jnp.dot(clo[g], got, preferred_element_type=F32)
                old = hx[g * half : (g + 1) * half].reshape(count, WIDE)
                new = (old.astype(F32) + added).astype(BF16)
                hx[g * half : (g + 1) * half] = new.reshape(half, tokens, WIDE)

        @pl.when(i <= last)
        def _():
            for g in range(2):
                x = hx[g * half : (g + 1) * half].reshape(count, WIDE)
                rows = jnp.dot(place[g], x, preferred_element_type=F32).astype(BF16)
                hrows[i, :, g * half * CAP : (g + 1) * half * CAP, :] = rows.reshape(
                    window, half * CAP, WIDE
                )

            def send(e, unused):
                self_copy = (layer == sec) & (e == exp)

                @pl.when(self_copy)
                def _():
                    pltpu.make_async_copy(
                        hrows.at[i, e // GROUP], ein.at[flow, sec], ein_sem.at[flow, sec]
                    ).start()

                @pl.when(jnp.logical_not(self_copy))
                def _():
                    pltpu.make_async_remote_copy(
                        src_ref=hrows.at[i, e // GROUP], dst_ref=ein.at[flow, sec],
                        send_sem=rows_sem.at[i], recv_sem=ein_sem.at[flow, sec],
                        device_id=(layer, e), device_id_type=MESH,
                    ).start()

                return unused

            lax.fori_loop(0, spread, send, 0)

        @pl.when(i > last)
        def _():
            def send(b, unused):
                @pl.when(b == exp)
                def _():
                    pltpu.make_async_copy(hx.at[b], fin.at[flow], fin_recv.at[flow]).start()

                @pl.when(b != exp)
                def _():
                    pltpu.make_async_remote_copy(
                        src_ref=hx.at[b], dst_ref=fin.at[flow],
                        send_sem=fin_send, recv_sem=fin_recv.at[flow],
                        device_id=(sec, b), device_id_type=MESH,
                    ).start()

                return unused

            lax.fori_loop(0, spread, send, 0)

    def expert_phase(f, i):
        gate = jnp.zeros((spread * CAP, hid), F32)
        up = jnp.zeros((spread * CAP, hid), F32)
        square = jnp.zeros((spread * CAP, WIDE), F32)
        for c in range(sections):
            pltpu.make_async_copy(ein.at[f, c], ein.at[f, c], ein_sem.at[f, c]).wait()
            x = ein[f, c].astype(F32)
            square += x * x
            h = (x * gain[c : c + 1, :]).astype(BF16)[:, :chunk]
            rows = slice(c * chunk, (c + 1) * chunk)
            gate += jnp.dot(h, wg[rows, :], preferred_element_type=F32)
            up += jnp.dot(h, wu[rows, :], preferred_element_type=F32)
        scale = lax.rsqrt(jnp.sum(square, axis=1, keepdims=True) / width + norm_eps)
        gate = gate * scale
        up = up * scale
        act[...] = (gate / (1.0 + jnp.exp(-gate)) * up).astype(BF16)
        sent = 0
        mine = lax.rem(exp, GROUP) * window + exp // GROUP
        for lo in range(0, width, 256):
            hi = min(lo + 256, width)
            part[:, lo:hi] = jnp.dot(act[...], wd[:, lo:hi], preferred_element_type=F32).astype(BF16)
            while sent < sections and (sent + 1) * chunk <= hi:
                c = sent
                eout[f, c, :, :chunk] = part[:, c * chunk : (c + 1) * chunk]
                home = home_of(f, jnp.int32(c))
                self_copy = (c == sec) & (home == exp)

                @pl.when(self_copy)
                def _():
                    pltpu.make_async_copy(eout.at[f, c], hparts.at[i, mine], parts_sem.at[i]).start()

                @pl.when(jnp.logical_not(self_copy))
                def _():
                    pltpu.make_async_remote_copy(
                        src_ref=eout.at[f, c], dst_ref=hparts.at[i, mine],
                        send_sem=eout_sem.at[f], recv_sem=parts_sem.at[i],
                        device_id=(c, home), device_id_type=MESH,
                    ).start()

                sent += 1

    def step(t, unused):
        i = t - micro

        @pl.when(is_home & (i >= 0) & (i <= sections))
        def _():
            home_phase(i)

        @pl.when(t == jnp.minimum(sec, last - sec))
        def _():
            for copy in weights:
                copy.wait()

        def direction(d, unused):
            at = jnp.where(d == 0, sec, last - sec)
            m = t - at

            @pl.when((m >= 0) & (m < 2))
            def _():
                expert_phase(d * 2 + m, at)

            return unused

        lax.fori_loop(0, 2, direction, 0)
        return unused

    lax.fori_loop(0, sections + 2, step, 0)

    for f in range(FLOWS):
        pltpu.make_async_copy(fin.at[f], fin.at[f], fin_recv.at[f]).wait()
        out[f] = fin[f][:, :chunk]

    one = hx.at[0]
    for f in range(FLOWS):
        home = home_of(f, sec)

        @pl.when(home == exp)
        def _():
            pltpu.make_async_copy(eout.at[f, 1:], eout.at[f, 1:], eout_sem.at[f]).wait()

        @pl.when(home != exp)
        def _():
            pltpu.make_async_copy(eout.at[f], eout.at[f], eout_sem.at[f]).wait()
            pltpu.make_async_copy(one, one, init_send.at[f]).wait()

    @pl.when(is_home)
    def _():
        def drain(i, unused):
            layer = jnp.where(way == 0, i, last - i)

            @pl.when(layer == sec)
            def _():
                some = hparts.at[i, 1:]
                pltpu.make_async_copy(some, some, rows_sem.at[i]).wait()

            @pl.when(layer != sec)
            def _():
                pltpu.make_async_copy(hparts.at[i], hparts.at[i], rows_sem.at[i]).wait()

            return unused

        lax.fori_loop(0, sections, drain, 0)
        pltpu.make_async_copy(hx.at[1:], hx.at[1:], fin_send).wait()


def slot_table(ids, scores):
    flows, tokens, _ = ids.shape
    window = lax.axis_size("expert") // GROUP
    weights = route_scale * scores / jnp.sum(scores, axis=-1, keepdims=True)
    hit = (ids[:, :, :, None] == jnp.arange(window, dtype=jnp.int32)).astype(F32)
    count = jnp.sum(hit, axis=2)
    share = jnp.sum(weights[:, :, :, None] * hit, axis=2)
    earlier = (jnp.arange(tokens)[:, None] > jnp.arange(tokens)[None, :]).astype(F32)
    before = jnp.sum(earlier[None, :, :, None] * count[:, None, :, :], axis=2)
    slot = jnp.arange(CAP, dtype=F32)
    place = count[..., None] * (before[..., None] == slot).astype(F32)
    number = jnp.arange(1, tokens + 1, dtype=F32)
    tok = jnp.sum(place * number[None, :, None, None], axis=1) - 1.0
    weight = jnp.sum(place * share[..., None], axis=1)
    return jnp.stack([tok, weight], axis=1).reshape(1, -1)


def on_device(entering, norm_gain, w_gate, w_up, w_down, route_ids, route_scores):
    sections = lax.axis_size("section")
    spread = lax.axis_size("expert")
    sec = lax.axis_index("section")
    tokens, width = entering.shape[2:]
    chunk = width // sections
    hid = w_gate.shape[2]
    pad = WIDE - chunk
    xin = lax.dynamic_slice_in_dim(entering, sec * chunk, chunk, 3).reshape(FLOWS, tokens, chunk)
    xin = jnp.pad(xin, ((0, 0), (0, 0), (0, pad)))
    gain = jnp.pad(norm_gain.reshape(sections, chunk), ((0, 0), (0, pad)))
    own = slot_table(
        route_ids[:, :, 0].reshape(FLOWS, tokens, -1), route_scores[:, :, 0].reshape(FLOWS, tokens, -1)
    )
    tab = lax.all_gather(own, ("section", "expert"), axis=0, tiled=True)
    slots = spread * CAP * spread // GROUP // 2
    count = spread // 2 * tokens
    vmem = pl.BlockSpec(memory_space=pltpu.VMEM)
    hbm = pl.BlockSpec(memory_space=pl.ANY)
    out = pl.pallas_call(
        kernel,
        out_shape=jax.ShapeDtypeStruct((FLOWS, tokens, chunk), BF16),
        in_specs=[vmem, vmem, vmem, hbm, hbm, hbm],
        out_specs=vmem,
        scratch_shapes=[
            pltpu.VMEM((width, hid), BF16),
            pltpu.VMEM((width, hid), BF16),
            pltpu.VMEM((hid, width), BF16),
            pltpu.VMEM((FLOWS, sections, spread * CAP, WIDE), BF16),
            pltpu.VMEM((FLOWS, sections, spread * CAP, WIDE), BF16),
            pltpu.VMEM((spread * CAP, width), BF16),
            pltpu.VMEM((spread * CAP, hid), BF16),
            pltpu.VMEM((spread, tokens, WIDE), BF16),
            pltpu.VMEM((sections, spread // GROUP, spread * CAP, WIDE), BF16),
            pltpu.VMEM((sections, spread, spread * CAP, WIDE), BF16),
            pltpu.VMEM((FLOWS, tokens, WIDE), BF16),
            pltpu.VMEM((sections * 2, slots), F32),
            pltpu.VMEM((sections * 2, slots), F32),
            pltpu.VMEM((slots, sections * 2), F32),
            pltpu.VMEM((2, count, 2 * slots), BF16),
            pltpu.VMEM((2, count, 2 * slots), BF16),
            pltpu.VMEM((2, slots, count), BF16),
            pltpu.SemaphoreType.DMA((3,)),
            pltpu.SemaphoreType.DMA((FLOWS,)),
            pltpu.SemaphoreType.DMA,
            pltpu.SemaphoreType.DMA((FLOWS, sections)),
            pltpu.SemaphoreType.DMA((FLOWS,)),
            pltpu.SemaphoreType.DMA((sections,)),
            pltpu.SemaphoreType.DMA((sections,)),
            pltpu.SemaphoreType.DMA,
            pltpu.SemaphoreType.DMA((FLOWS,)),
        ],
        compiler_params=pltpu.CompilerParams(
            has_side_effects=True, vmem_limit_bytes=48 * 2**20
        ),
        cost_estimate=pl.CostEstimate(
            flops=2 * FLOWS * spread * CAP * width * hid * 3,
            bytes_accessed=width * hid * 6,
            transcendentals=0,
        ),
        name="relay",
    )(xin, gain, tab, w_gate[0], w_up[0], w_down[0])
    return out.reshape(2, 2, tokens, chunk)


def solution(mesh):
    return jax.shard_map(
        on_device,
        mesh=mesh,
        in_specs=(
            P(None, None, "expert", None),
            P("section", None),
            P("section", None, "expert"),
            P("section", None, "expert"),
            P("section", "expert", None),
            P(None, None, "section", "expert", None),
            P(None, None, "section", "expert", None),
        ),
        out_specs=P(None, None, "expert", "section"),
        check_vma=False,
    )
```

```python
import jax
import jax.numpy as jnp
from jax import lax
from jax.experimental import pallas as pl
from jax.experimental.pallas import tpu as pltpu
from jax.sharding import PartitionSpec as P

MESH = pl.DeviceIdType.MESH
BF16, F32 = jnp.bfloat16, jnp.float32

GROUP = 2
CAP = 2
FLOWS = 4
WIDE = 256
NZ = 4
NY = 4

norm_eps = 1e-06
route_scale = 2.5


def home_of(flow, x, y):
    return lax.rem(x + y + flow // 2, 2) * (2 * NY) + y * 2 + flow % 2


def iota(shape, dim):
    return lax.broadcasted_iota(jnp.int32, shape, dim)


def kernel(
    entering, norm_gain, wg_h, wu_h, wd_h, ids, scores, out,
    wg, wu, wd, raw, xin, gain, ein, eout, part, act,
    hx, hnew, hrows, hparts, fin, tabrow, tab, chi, clo, place,
    w_sem, raw_sem, init_send, init_recv, ein_sem, eout_sem, rows_sem, parts_sem,
    move_send, move_recv, fin_send, fin_recv, tab_send, tab_recv,
):
    sections = lax.axis_size("section")
    spread = lax.axis_size("expert")
    window = spread // GROUP
    nx = sections // NZ
    sec, exp = lax.axis_index("section"), lax.axis_index("expert")
    my_x, my_z = sec // NZ, lax.rem(sec, NZ)
    my_y = lax.rem(exp // 2, NY)
    tokens = ids.shape[3]
    width = wg_h.shape[1]
    chunk = width // sections
    block = chunk * NY
    hid = wg_h.shape[2]
    last = sections - 1
    half = spread // 2
    slots = half * CAP * window
    count = half * tokens

    flow = lax.rem(exp // (2 * NY) + my_x + my_y, 2) * 2 + lax.rem(exp, 2)
    way = flow // 2
    my_chunk = my_x * NY + my_y
    starts = my_z == way * (NZ - 1)
    ends = my_z == (1 - way) * (NZ - 1)
    first_visit = way * (nx - 1)

    def send(src, dst, send_sem, recv_sem, section, device):
        here = (section == sec) & (device == exp)

        @pl.when(here)
        def _():
            pltpu.make_async_copy(src, dst, recv_sem).start()

        @pl.when(jnp.logical_not(here))
        def _():
            pltpu.make_async_remote_copy(
                src_ref=src, dst_ref=dst, send_sem=send_sem, recv_sem=recv_sem,
                device_id=(section, device), device_id_type=MESH,
            ).start()

    def sent(src, send_sem, section, device):
        @pl.when(jnp.logical_not((section == sec) & (device == exp)))
        def _():
            pltpu.make_async_copy(src, src, send_sem).wait()

    def arrived(ref, sem):
        pltpu.make_async_copy(ref, ref, sem).wait()

    mine_in = entering.at[:, :, :, pl.ds(pl.multiple_of(my_x * block, 128), block)]
    fetch = pltpu.make_async_copy(mine_in, raw, raw_sem)
    fetch.start()
    weights = [
        pltpu.make_async_copy(src.at[0], dst, w_sem.at[k])
        for k, (src, dst) in enumerate(((wg_h, wg), (wu_h, wu), (wd_h, wd)))
    ]

    lanes = FLOWS * 2 * window * CAP
    lane = iota((1, lanes), 1)
    lane_expert = lax.rem(lane // CAP, window)
    lane_slot = lax.rem(lane, CAP).astype(F32)
    lane_kind = lax.rem(lane // (CAP * window), 2)
    lane_flow = lane // (2 * CAP * window)
    earlier = (iota((tokens, tokens), 0) > iota((tokens, tokens), 1)).astype(BF16)
    number = iota((tokens, lanes), 0).astype(F32) + 1.0
    table = jnp.zeros((1, lanes), F32)
    for f in range(FLOWS):
        chosen = ids[f // 2, f % 2, 0]
        score = scores[f // 2, f % 2, 0]
        weight = route_scale * score / jnp.sum(score, axis=1, keepdims=True)
        hit = jnp.zeros((tokens, lanes), F32)
        share = jnp.zeros((tokens, lanes), F32)
        for k in range(chosen.shape[1]):
            same = chosen[:, k : k + 1] == lane_expert
            hit += jnp.where(same, 1.0, 0.0)
            share += jnp.where(same, weight[:, k : k + 1], 0.0)
        before = jnp.dot(earlier, hit.astype(BF16), preferred_element_type=F32)
        held = jnp.where(before == lane_slot, hit, 0.0)
        value = jnp.where(lane_kind == 0, number, share)
        row = jnp.sum(held * value, axis=0, keepdims=True) - jnp.where(lane_kind == 0, 1.0, 0.0)
        table += jnp.where(lane_flow == f, row, 0.0)
    tabrow[0] = table

    def tables(deliver):
        for f in range(FLOWS):
            d = f // 2
            prior = sec + (2 * d - 1)

            def one(c, unused):
                x, y = c // NY, lax.rem(c, NY)
                device = home_of(f, x, y)

                @pl.when(sec == d * last)
                def _():
                    deliver(2 * nx, x * NZ + my_z, device)

                @pl.when((prior >= 0) & (prior <= last))
                def _():
                    deliver(nx + prior // NZ, x * NZ + lax.rem(prior, NZ), device)

                deliver(my_x, x * NZ + my_z, device)
                return unused

            lax.fori_loop(0, sections, one, 0)

    def deliver_table(use, section, device):
        send(tabrow.at[0], tab.at[use, exp], tab_send, tab_recv.at[use], section, device)

    def drain_table(use, section, device):
        sent(tabrow.at[0], tab_send, section, device)

    fetch.wait()

    def enter(act_on):
        for f in range(FLOWS):
            d, m = f // 2, f % 2

            @pl.when(my_z == d * (NZ - 1))
            def _():
                for y in range(NY):
                    act_on(f, d, m, y, home_of(f, my_x, y))

    def send_entering(f, d, m, y, device):
        xin[m, y] = jnp.zeros((tokens, WIDE), BF16)
        xin[m, y, :, :chunk] = raw[d, m, :, y * chunk : (y + 1) * chunk]
        send(xin.at[m, y], hx.at[d * (nx - 1), exp], init_send.at[m, y], init_recv, sec, device)

    def sent_entering(f, d, m, y, device):
        sent(xin.at[m, y], init_send.at[m, y], sec, device)

    enter(send_entering)
    tables(deliver_table)
    for copy in weights:
        copy.start()
    eout[...] = jnp.zeros_like(eout)
    for c in range(sections):
        gain[c : c + 1, :] = jnp.zeros((1, WIDE), F32)
        gain[c : c + 1, :chunk] = norm_gain[:, c * chunk : (c + 1) * chunk]

    spot = iota((1, slots), 1)
    spot_lane = (spot // (half * CAP)) * CAP + lax.rem(spot, CAP)
    spot_block = lax.rem(spot // CAP, half)

    def pick(kind):
        return (iota((lanes, slots), 0) == (flow * 2 + kind) * (window * CAP) + spot_lane).astype(F32)

    def rows_of(use, kind):
        got = jnp.concatenate([tab[use, b] for b in range(spread)], axis=0)
        wide = jnp.dot(got, pick(kind), precision=lax.Precision.HIGHEST, preferred_element_type=F32)
        own = lax.rem(iota((spread, slots), 0), half) == spot_block
        kept = jnp.where(own, wide, 0.0)
        return [jnp.sum(kept[g * half : (g + 1) * half], axis=0, keepdims=True) for g in range(2)]

    def prepare_sums(use):
        arrived(tab.at[use], tab_recv.at[use])
        toks, shares = rows_of(use, 0), rows_of(use, 1)
        for g in range(2):
            tok = jnp.where(toks[g] < -0.5, -1.0, toks[g] + (spot_block * tokens).astype(F32))
            comb = jnp.where(iota((count, slots), 0).astype(F32) == tok, shares[g], 0.0)
            high = comb.astype(BF16)
            low = (comb - high.astype(F32)).astype(BF16)
            chi[g] = jnp.concatenate([high, high], axis=1)
            clo[g] = jnp.concatenate([low, low], axis=1)

    def prepare_rows(use):
        arrived(tab.at[use], tab_recv.at[use])
        toks = rows_of(use, 0)
        for g in range(2):
            tok = jnp.where(toks[g] < -0.5, -1.0, toks[g] + (spot_block * tokens).astype(F32))
            col = jnp.broadcast_to(tok, (slots, slots)).T[:, :1]
            place[g] = (iota((slots, count), 1).astype(F32) == col).astype(BF16)

    def dispatch(source, k, layer):
        for g in range(2):
            x = source[g * half : (g + 1) * half].reshape(count, WIDE)
            rows = jnp.dot(place[g], x, preferred_element_type=F32).astype(BF16)
            hrows[k, :, g * half * CAP : (g + 1) * half * CAP, :] = rows.reshape(
                window, half * CAP, WIDE
            )

        def one(e, unused):
            send(
                hrows.at[k, e // GROUP], ein.at[flow, my_chunk],
                rows_sem.at[k], ein_sem.at[flow, my_chunk], layer, e,
            )
            return unused

        lax.fori_loop(0, spread, one, 0)

    @pl.when(starts)
    def _():
        prepare_rows(2 * nx)
        arrived(hx.at[first_visit], init_recv)
        dispatch(hx[first_visit], nx, way * last)

    tables(drain_table)
    enter(sent_entering)

    around = sorted(
        ((dx, dy) for dx in range(nx) for dy in range(NY)),
        key=lambda o: (min(o[0], nx - o[0]) + min(o[1], NY - o[1]), o),
    )
    columns = sorted(range(nx), key=lambda dx: -min(dx, nx - dx))

    def expert_phase(f):
        gate = jnp.zeros((spread * CAP, hid), F32)
        up = jnp.zeros((spread * CAP, hid), F32)
        square = jnp.zeros((spread * CAP, WIDE), F32)
        for dx, dy in around:
            c = lax.rem(my_x + dx, nx) * NY + lax.rem(my_y + dy, NY)
            arrived(ein.at[f, c], ein_sem.at[f, c])
            x = ein[f, c].astype(F32)
            square += x * x
            h = (x * gain[pl.ds(c, 1), :]).astype(BF16)[:, :chunk]
            rows = pl.ds(pl.multiple_of(c * chunk, 32), chunk)
            gate += jnp.dot(h, wg[rows, :], preferred_element_type=F32)
            up += jnp.dot(h, wu[rows, :], preferred_element_type=F32)
        scale = lax.rsqrt(jnp.sum(square, axis=1, keepdims=True) / width + norm_eps)
        gate = gate * scale
        up = up * scale
        act[...] = (gate / (1.0 + jnp.exp(-gate)) * up).astype(BF16)
        mine = lax.rem(exp, GROUP) * window + exp // GROUP
        for dx in columns:
            x = lax.rem(my_x + dx, nx)
            cols = pl.ds(pl.multiple_of(x * block, 128), block)
            part[...] = jnp.dot(act[...], wd[:, cols], preferred_element_type=F32).astype(BF16)
            for y in range(NY):
                c = x * NY + y
                eout[f, c, :, :chunk] = part[:, y * chunk : (y + 1) * chunk]
                send(
                    eout.at[f, c], hparts.at[my_x, mine], eout_sem.at[f], parts_sem.at[my_x],
                    x * NZ + my_z, home_of(f, x, y),
                )

    def home_phase(k, layer):
        following = layer + 1 - 2 * way
        onward = (following >= 0) & (following <= last)
        prepare_sums(k)

        @pl.when(onward)
        def _():
            prepare_rows(nx + k)

        @pl.when(jnp.logical_not(starts & (k == first_visit)))
        def _():
            arrived(hx.at[k], move_recv.at[k])

        arrived(hparts.at[k], parts_sem.at[k])
        for g in range(2):
            got = hparts[k, :, g * half * CAP : (g + 1) * half * CAP, :]
            got = got.reshape(2 * slots, WIDE)
            added = jnp.dot(chi[g], got, preferred_element_type=F32)
            added += jnp.dot(clo[g], got, preferred_element_type=F32)
            old = hx[k, g * half : (g + 1) * half].reshape(count, WIDE)
            new = (old.astype(F32) + added).astype(BF16)
            hnew[k, g * half : (g + 1) * half] = new.reshape(half, tokens, WIDE)

        @pl.when(onward)
        def _():
            dispatch(hnew[k], k, following)
            pltpu.make_async_remote_copy(
                src_ref=hnew.at[k], dst_ref=hx.at[following // NZ],
                send_sem=move_send.at[k], recv_sem=move_recv.at[following // NZ],
                device_id=(my_x * NZ + lax.rem(following, NZ), exp), device_id_type=MESH,
            ).start()

        @pl.when(jnp.logical_not(onward))
        def _():
            def one(b, unused):
                send(hnew.at[k, b], fin.at[flow], fin_send, fin_recv.at[flow], my_chunk, b)
                return unused

            lax.fori_loop(0, spread, one, 0)

    def step(t, unused):
        @pl.when(t == jnp.minimum(sec, last - sec))
        def _():
            for copy in weights:
                copy.wait()

        def direction(d, unused):
            @pl.when(t == jnp.where(d == 0, sec, last - sec))
            def _():
                def micro(m, unused):
                    expert_phase(d * 2 + m)
                    return unused

                lax.fori_loop(0, 2, micro, 0)

            return unused

        lax.fori_loop(0, 2, direction, 0)
        layer = jnp.where(way == 0, t, last - t)

        @pl.when(lax.rem(layer, NZ) == my_z)
        def _():
            home_phase(layer // NZ, layer)

        return unused

    lax.fori_loop(0, sections, step, 0)

    for f in range(FLOWS):

        @pl.when(f == flow)
        def _():
            arrived(eout.at[f, 1:], eout_sem.at[f])

        @pl.when(f != flow)
        def _():
            arrived(eout.at[f], eout_sem.at[f])

    for k in range(nx):
        final = ends & (k == (1 - way) * (nx - 1))

        @pl.when(jnp.logical_not(final))
        def _():
            arrived(hparts.at[k], rows_sem.at[k])
            arrived(hnew.at[k], move_send.at[k])

        @pl.when(final)
        def _():
            lax.fori_loop(
                0, spread, lambda b, unused: (sent(hnew.at[k, 0], fin_send, my_chunk, b), unused)[1], 0
            )

    @pl.when(starts)
    def _():
        lax.fori_loop(
            0, spread, lambda e, unused: (sent(hrows.at[nx, 0], rows_sem.at[nx], way * last, e), unused)[1], 0
        )

    for f in range(FLOWS):
        arrived(fin.at[f], fin_recv.at[f])
        out[f // 2, f % 2] = fin[f][:, :chunk]


def on_device(entering, norm_gain, w_gate, w_up, w_down, route_ids, route_scores):
    sections = lax.axis_size("section")
    spread = lax.axis_size("expert")
    tokens, width = entering.shape[2:]
    chunk = width // sections
    hid = w_gate.shape[2]
    nx = sections // NZ
    window = spread // GROUP
    rows = spread * CAP
    slots = spread // 2 * CAP * window
    count = spread // 2 * tokens
    lanes = FLOWS * 2 * window * CAP
    vmem = pl.BlockSpec(memory_space=pltpu.VMEM)
    hbm = pl.BlockSpec(memory_space=pl.ANY)
    dma = pltpu.SemaphoreType.DMA
    return pl.pallas_call(
        kernel,
        out_shape=jax.ShapeDtypeStruct((2, 2, tokens, chunk), BF16),
        in_specs=[hbm, vmem, hbm, hbm, hbm, vmem, vmem],
        out_specs=vmem,
        scratch_shapes=[
            pltpu.VMEM((width, hid), BF16),
            pltpu.VMEM((width, hid), BF16),
            pltpu.VMEM((hid, width), BF16),
            pltpu.VMEM((2, 2, tokens, chunk * NY), BF16),
            pltpu.VMEM((2, NY, tokens, WIDE), BF16),
            pltpu.VMEM((sections, WIDE), F32),
            pltpu.VMEM((FLOWS, sections, rows, WIDE), BF16),
            pltpu.VMEM((FLOWS, sections, rows, WIDE), BF16),
            pltpu.VMEM((rows, chunk * NY), BF16),
            pltpu.VMEM((rows, hid), BF16),
            pltpu.VMEM((nx, spread, tokens, WIDE), BF16),
            pltpu.VMEM((nx, spread, tokens, WIDE), BF16),
            pltpu.VMEM((nx + 1, window, rows, WIDE), BF16),
            pltpu.VMEM((nx, spread, rows, WIDE), BF16),
            pltpu.VMEM((FLOWS, tokens, WIDE), BF16),
            pltpu.VMEM((1, 1, lanes), F32),
            pltpu.VMEM((2 * nx + 1, spread, 1, lanes), F32),
            pltpu.VMEM((2, count, 2 * slots), BF16),
            pltpu.VMEM((2, count, 2 * slots), BF16),
            pltpu.VMEM((2, slots, count), BF16),
            dma((3,)),
            dma,
            dma((2, NY)),
            dma,
            dma((FLOWS, sections)),
            dma((FLOWS,)),
            dma((nx + 1,)),
            dma((nx,)),
            dma((nx,)),
            dma((nx,)),
            dma,
            dma((FLOWS,)),
            dma,
            dma((2 * nx + 1,)),
        ],
        compiler_params=pltpu.CompilerParams(
            has_side_effects=True, vmem_limit_bytes=48 * 2**20
        ),
        cost_estimate=pl.CostEstimate(
            flops=2 * FLOWS * rows * width * hid * 3,
            bytes_accessed=width * hid * 6,
            transcendentals=0,
        ),
        name="relay",
    )(entering, norm_gain, w_gate, w_up, w_down, route_ids, route_scores)


def solution(mesh):
    return jax.shard_map(
        on_device,
        mesh=mesh,
        in_specs=(
            P(None, None, "expert", None),
            P("section", None),
            P("section", None, "expert"),
            P("section", None, "expert"),
            P("section", "expert", None),
            P(None, None, "section", "expert", None),
            P(None, None, "section", "expert", None),
        ),
        out_specs=P(None, None, "expert", "section"),
        check_vma=False,
    )
```

```python
import jax
import jax.numpy as jnp
from jax import lax
from jax.experimental import pallas as pl
from jax.experimental.pallas import tpu as pltpu
from jax.sharding import PartitionSpec as P

MESH = pl.DeviceIdType.MESH
BF16, F32 = jnp.bfloat16, jnp.float32

GROUP = 2
CAP = 2
FLOWS = 4
WIDE = 256
NZ = 4
NY = 4
FAR = 9

norm_eps = 1e-06
route_scale = 2.5


def home_of(flow, x, y):
    return lax.rem(x + y + flow // 2, 2) * (2 * NY) + y * 2 + flow % 2


def iota(shape, dim):
    return lax.broadcasted_iota(jnp.int32, shape, dim)


def kernel(
    entering, gain_h, wg_h, wu_h, wd_h, ids_h, scores_h, out,
    wg, wu, wd, raw, xin, gain, ein, eout, part, act,
    hx, hnew, hrows, hparts, fin, tabrow, tab, chi, clo, place,
    turn, norm_gain, ids, scores, gain_sem, eswap, pin, swap_send, pin_sem, pass_send,
    w_sem, raw_sem, init_send, init_recv, ein_sem, eout_sem, rows_sem, parts_sem,
    move_send, move_recv, fin_send, fin_recv, tab_send, tab_recv,
):
    sections = lax.axis_size("section")
    spread = lax.axis_size("expert")
    window = spread // GROUP
    nx = sections // NZ
    sec, exp = lax.axis_index("section"), lax.axis_index("expert")
    my_x, my_z = sec // NZ, lax.rem(sec, NZ)
    my_y = lax.rem(exp // 2, NY)
    tokens = ids.shape[4]
    width = wg_h.shape[1]
    chunk = width // sections
    block = chunk * NY
    hid = wg_h.shape[2]
    last = sections - 1
    half = spread // 2
    slots = half * CAP * window
    count = half * tokens

    flow = lax.rem(exp // (2 * NY) + my_x + my_y, 2) * 2 + lax.rem(exp, 2)
    way = flow // 2
    my_chunk = my_x * NY + my_y
    starts = my_z == way * (NZ - 1)
    ends = my_z == (1 - way) * (NZ - 1)
    first_visit = way * (nx - 1)

    def send(src, dst, send_sem, recv_sem, section, device):
        here = (section == sec) & (device == exp)

        @pl.when(here)
        def _():
            pltpu.make_async_copy(src, dst, recv_sem).start()

        @pl.when(jnp.logical_not(here))
        def _():
            pltpu.make_async_remote_copy(
                src_ref=src, dst_ref=dst, send_sem=send_sem, recv_sem=recv_sem,
                device_id=(section, device), device_id_type=MESH,
            ).start()

    def sent(src, send_sem, section, device):
        @pl.when(jnp.logical_not((section == sec) & (device == exp)))
        def _():
            pltpu.make_async_copy(src, src, send_sem).wait()

    def arrived(ref, sem):
        pltpu.make_async_copy(ref, ref, sem).wait()

    mine_in = entering.at[:, :, :, pl.ds(pl.multiple_of(my_x * block, 128), block)]
    fetch = pltpu.make_async_copy(mine_in, raw, raw_sem)
    small = [
        pltpu.make_async_copy(src, dst, gain_sem.at[k])
        for k, (src, dst) in enumerate(((ids_h, ids), (scores_h, scores), (gain_h, norm_gain)))
    ]
    for copy in small:
        copy.start()
    fetch.start()
    weights = [
        pltpu.make_async_copy(src.at[0], dst, w_sem.at[k])
        for k, (src, dst) in enumerate(((wg_h, wg), (wu_h, wu), (wd_h, wd)))
    ]

    for copy in weights:
        copy.start()
    for copy in small:
        copy.wait()

    lanes = FLOWS * 2 * window * CAP
    lane = iota((1, lanes), 1)
    lane_expert = lax.rem(lane // CAP, window)
    lane_slot = lax.rem(lane, CAP).astype(F32)
    lane_kind = lax.rem(lane // (CAP * window), 2)
    lane_flow = lane // (2 * CAP * window)
    earlier = (iota((tokens, tokens), 0) > iota((tokens, tokens), 1)).astype(BF16)
    number = iota((tokens, lanes), 0).astype(F32) + 1.0
    table = jnp.zeros((1, lanes), F32)
    for f in range(FLOWS):
        chosen = ids[f // 2, f % 2, 0].T
        score = scores[f // 2, f % 2, 0].T
        weight = route_scale * score / jnp.sum(score, axis=1, keepdims=True)
        hit = jnp.zeros((tokens, lanes), F32)
        share = jnp.zeros((tokens, lanes), F32)
        for k in range(chosen.shape[1]):
            same = chosen[:, k : k + 1] == lane_expert
            hit += jnp.where(same, 1.0, 0.0)
            share += jnp.where(same, weight[:, k : k + 1], 0.0)
        before = jnp.dot(earlier, hit.astype(BF16), preferred_element_type=F32)
        held = jnp.where(before == lane_slot, hit, 0.0)
        value = jnp.where(lane_kind == 0, number, share)
        row = jnp.sum(held * value, axis=0, keepdims=True) - jnp.where(lane_kind == 0, 1.0, 0.0)
        table += jnp.where(lane_flow == f, row, 0.0)
    tabrow[0] = table

    def tables(deliver, first):
        for f in range(FLOWS):
            d = f // 2
            prior = sec + (2 * d - 1)

            def one(c, unused):
                x, y = c // NY, lax.rem(c, NY)
                device = home_of(f, x, y)

                if first:
                    deliver(2 * nx, x * NZ + my_z, device)
                    return unused

                @pl.when((prior >= 0) & (prior <= last))
                def _():
                    deliver(nx + prior // NZ, x * NZ + lax.rem(prior, NZ), device)

                deliver(my_x, x * NZ + my_z, device)
                return unused

            if first:

                @pl.when(sec == d * last)
                def _():
                    lax.fori_loop(0, sections, one, 0)

            else:
                lax.fori_loop(0, sections, one, 0)

    def deliver_table(use, section, device):
        send(tabrow.at[0], tab.at[use, exp], tab_send, tab_recv.at[use], section, device)

    def drain_table(use, section, device):
        sent(tabrow.at[0], tab_send, section, device)

    tables(deliver_table, True)
    fetch.wait()

    def enter(act_on):
        for f in range(FLOWS):
            d, m = f // 2, f % 2

            @pl.when(my_z == d * (NZ - 1))
            def _():
                for y in range(NY):
                    act_on(f, d, m, y, home_of(f, my_x, y))

    def send_entering(f, d, m, y, device):
        xin[m, y] = jnp.zeros((tokens, WIDE), BF16)
        xin[m, y, :, :chunk] = raw[d, m, :, y * chunk : (y + 1) * chunk]
        send(xin.at[m, y], hx.at[d * (nx - 1), exp], init_send.at[m, y], init_recv, sec, device)

    def sent_entering(f, d, m, y, device):
        sent(xin.at[m, y], init_send.at[m, y], sec, device)

    enter(send_entering)
    spot = iota((1, slots), 1)
    spot_lane = (spot // (half * CAP)) * CAP + lax.rem(spot, CAP)
    spot_block = lax.rem(spot // CAP, half)

    def pick(kind):
        return (iota((lanes, slots), 0) == (flow * 2 + kind) * (window * CAP) + spot_lane).astype(F32)

    def rows_of(use, kind):
        got = jnp.concatenate([tab[use, b] for b in range(spread)], axis=0)
        wide = jnp.dot(got, pick(kind), precision=lax.Precision.HIGHEST, preferred_element_type=F32)
        own = lax.rem(iota((spread, slots), 0), half) == spot_block
        kept = jnp.where(own, wide, 0.0)
        return [jnp.sum(kept[g * half : (g + 1) * half], axis=0, keepdims=True) for g in range(2)]

    def prepare_sums(use):
        arrived(tab.at[use], tab_recv.at[use])
        toks, shares = rows_of(use, 0), rows_of(use, 1)
        for g in range(2):
            tok = jnp.where(toks[g] < -0.5, -1.0, toks[g] + (spot_block * tokens).astype(F32))
            comb = jnp.where(iota((count, slots), 0).astype(F32) == tok, shares[g], 0.0)
            high = comb.astype(BF16)
            low = (comb - high.astype(F32)).astype(BF16)
            chi[g] = high
            clo[g] = low

    def prepare_rows(use):
        arrived(tab.at[use], tab_recv.at[use])
        toks = rows_of(use, 0)
        for g in range(2):
            tok = jnp.where(toks[g] < -0.5, -1.0, toks[g] + (spot_block * tokens).astype(F32))
            col = jnp.broadcast_to(tok, (slots, slots)).T[:, :1]
            place[g] = (iota((slots, count), 1).astype(F32) == col).astype(BF16)

    def far_from(x, y):
        dx = lax.rem(my_x - x + nx, nx)
        dy = lax.rem(my_y - y + NY, NY)
        return jnp.minimum(dx, nx - dx) + jnp.minimum(dy, NY - dy) >= FAR

    def rows_to(k, layer, act_on):
        def one(i, unused):
            e = lax.rem(i + (my_y + 1) * 2, 2 * NY) + (i // (2 * NY)) * 2 * NY
            takes = lax.rem(e, 2) == lax.rem(my_y, 2)

            @pl.when(takes | far_from(layer // NZ, lax.rem(e // 2, NY)))
            def _():
                act_on(
                    hrows.at[k, e // GROUP], ein.at[flow, my_chunk],
                    rows_sem.at[k], ein_sem.at[flow, my_chunk], layer, e,
                )

            return unused

        lax.fori_loop(0, spread, one, 0)

    def drain_rows(src, dst, send_sem, recv_sem, section, device):
        sent(src, send_sem, section, device)

    def dispatch(source, k, layer):
        for g in range(2):
            x = source[g * half : (g + 1) * half].reshape(count, WIDE)
            rows = jnp.dot(place[g], x, preferred_element_type=F32).astype(BF16)
            hrows[k, :, g * half * CAP : (g + 1) * half * CAP, :] = rows.reshape(
                window, half * CAP, WIDE
            )

        rows_to(k, layer, send)


    @pl.when(starts)
    def _():
        prepare_rows(2 * nx)
        arrived(hx.at[first_visit], init_recv)
        dispatch(hx[first_visit], nx, way * last)

    tables(deliver_table, False)
    eout[...] = jnp.zeros_like(eout)
    eswap[...] = jnp.zeros_like(eswap)
    for c in range(sections):
        gain[c : c + 1, :] = jnp.zeros((1, WIDE), F32)
        gain[c : c + 1, :chunk] = norm_gain[:, c * chunk : (c + 1) * chunk]
    tables(drain_table, True)
    tables(drain_table, False)
    enter(sent_entering)

    around = sorted(
        ((dx, dy) for dx in range(nx) for dy in range(NY // 2)),
        key=lambda o: (min(o[0], nx - o[0]) + 2 * o[1], o),
    )
    core = lax.rem(exp, 2)
    sibling = exp + 1 - 2 * core
    columns = sorted(range(nx), key=lambda dx: -min(dx, nx - dx))

    def expert_phase(f):
        gate = jnp.zeros((spread * CAP, hid), F32)
        up = jnp.zeros((spread * CAP, hid), F32)
        square = jnp.zeros((spread * CAP, WIDE), F32)
        for passes in (True, False):
            for dx, half_dy in around:
                odd = lax.rem(my_y + core, 2) if passes else lax.rem(my_y + core + 1, 2)
                y = lax.rem(my_y + 2 * half_dy + odd, NY)
                c = lax.rem(my_x + dx, nx) * NY + y
                arrived(ein.at[f, c], ein_sem.at[f, c])
                if passes:

                    @pl.when(jnp.logical_not(far_from(lax.rem(my_x + dx, nx), y)))
                    def _():
                        pltpu.make_async_remote_copy(
                            src_ref=ein.at[f, c], dst_ref=ein.at[f, c],
                            send_sem=pass_send.at[f], recv_sem=ein_sem.at[f, c],
                            device_id=(sec, sibling), device_id_type=MESH,
                        ).start()

                x = ein[f, c].astype(F32)
                square += x * x
                h = (x * gain[pl.ds(c, 1), :]).astype(BF16)[:, :chunk]
                rows = pl.ds(pl.multiple_of(c * chunk, 32), chunk)
                gate += jnp.dot(h, wg[rows, :], preferred_element_type=F32)
                up += jnp.dot(h, wu[rows, :], preferred_element_type=F32)
        scale = lax.rsqrt(jnp.sum(square, axis=1, keepdims=True) / width + norm_eps)
        gate = gate * scale
        up = up * scale
        act[...] = (gate / (1.0 + jnp.exp(-gate)) * up).astype(BF16)
        for n, dx in enumerate(columns):
            x = lax.rem(my_x + dx, nx)
            cols = pl.ds(pl.multiple_of(x * block, 128), block)
            part[n] = jnp.dot(act[...], wd[:, cols], preferred_element_type=F32).astype(BF16)
            for y in range(NY):

                @pl.when(core != y % 2)
                def _():
                    c = x * NY + y
                    eswap[f, x, y // 2, :, :chunk] = part[n, :, y * chunk : (y + 1) * chunk]
                    pltpu.make_async_remote_copy(
                        src_ref=eswap.at[f, x, y // 2], dst_ref=pin.at[f, x, y // 2],
                        send_sem=swap_send.at[f], recv_sem=pin_sem.at[f, c],
                        device_id=(sec, sibling), device_id_type=MESH,
                    ).start()

        for n, dx in enumerate(columns):
            x = lax.rem(my_x + dx, nx)
            for y in range(NY):

                @pl.when(core == y % 2)
                def _():
                    c = x * NY + y
                    arrived(pin.at[f, x, y // 2], pin_sem.at[f, c])
                    own = part[n, :, y * chunk : (y + 1) * chunk].astype(F32)
                    other = pin[f, x, y // 2, :, :chunk].astype(F32)
                    eout[f, x, y // 2, :, :chunk] = (own + other).astype(BF16)
                    send(
                        eout.at[f, x, y // 2], hparts.at[my_x, exp // GROUP], eout_sem.at[f],
                        parts_sem.at[my_x], x * NZ + my_z, home_of(f, x, y),
                    )

    def home_phase(k, layer):
        following = layer + 1 - 2 * way
        onward = (following >= 0) & (following <= last)
        prepare_sums(k)

        @pl.when(onward)
        def _():
            prepare_rows(nx + k)

        @pl.when(jnp.logical_not(starts & (k == first_visit)))
        def _():
            arrived(hx.at[k], move_recv.at[k])

        arrived(hparts.at[k], parts_sem.at[k])
        for g in range(2):
            got = hparts[k, :, g * half * CAP : (g + 1) * half * CAP, :]
            got = got.reshape(slots, WIDE)
            added = jnp.dot(chi[g], got, preferred_element_type=F32)
            added += jnp.dot(clo[g], got, preferred_element_type=F32)
            old = hx[k, g * half : (g + 1) * half].reshape(count, WIDE)
            new = (old.astype(F32) + added).astype(BF16)
            hnew[k, g * half : (g + 1) * half] = new.reshape(half, tokens, WIDE)

        @pl.when(onward)
        def _():
            dispatch(hnew[k], k, following)

            pltpu.make_async_remote_copy(
                src_ref=hnew.at[k], dst_ref=hx.at[following // NZ],
                send_sem=move_send.at[k], recv_sem=move_recv.at[following // NZ],
                device_id=(my_x * NZ + lax.rem(following, NZ), exp), device_id_type=MESH,
            ).start()

        @pl.when(jnp.logical_not(onward))
        def _():
            def one(b, unused):
                send(hnew.at[k, b], fin.at[flow], fin_send, fin_recv.at[flow], my_chunk, b)
                return unused

            lax.fori_loop(0, spread, one, 0)

    def step(t, unused):
        @pl.when(t == jnp.minimum(sec, last - sec))
        def _():
            for copy in weights:
                copy.wait()

        def direction(d, unused):
            @pl.when(t == jnp.where(d == 0, sec, last - sec))
            def _():
                def micro(m, unused):
                    expert_phase(d * 2 + m)
                    return unused

                lax.fori_loop(0, 2, micro, 0)

            return unused

        lax.fori_loop(0, 2, direction, 0)
        layer = jnp.where(way == 0, t, last - t)

        @pl.when(lax.rem(layer, NZ) == my_z)
        def _():
            home_phase(layer // NZ, layer)

        return unused

    lax.fori_loop(0, sections, step, 0)

    for f in range(FLOWS):
        arrived(eswap.at[f], swap_send.at[f])
        inner = [
            (dx, dy) for dx in range(nx) for dy in range(NY)
            if min(dx, nx - dx) + min(dy, NY - dy) < FAR
        ]
        for parity in range(2):
            passed = sum(1 for _, dy in inner if dy % 2 == parity)

            @pl.when(lax.rem(my_y + core, 2) == parity)
            def _():
                arrived(ein.at[f, :passed], pass_send.at[f])

        own = (f == flow) & (core == lax.rem(my_y, 2))

        @pl.when(own)
        def _():
            arrived(ein.at[f, 1 : sections // 2], eout_sem.at[f])

        @pl.when(jnp.logical_not(own))
        def _():
            arrived(ein.at[f, : sections // 2], eout_sem.at[f])

    for k in range(nx):
        final = ends & (k == (1 - way) * (nx - 1))

        @pl.when(jnp.logical_not(final))
        def _():
            rows_to(k, NZ * k + my_z + 1 - 2 * way, drain_rows)
            arrived(hnew.at[k], move_send.at[k])

        @pl.when(final)
        def _():
            lax.fori_loop(
                0, spread, lambda b, unused: (sent(hnew.at[k, 0], fin_send, my_chunk, b), unused)[1], 0
            )

    @pl.when(starts)
    def _():
        rows_to(nx, way * last, drain_rows)

    for f in range(FLOWS):
        arrived(fin.at[f], fin_recv.at[f])
        out[f // 2, f % 2] = fin[f][:, :chunk]


def on_device(entering, norm_gain, w_gate, w_up, w_down, route_ids, route_scores):
    sections = lax.axis_size("section")
    spread = lax.axis_size("expert")
    tokens, width = entering.shape[2:]
    chunk = width // sections
    hid = w_gate.shape[2]
    nx = sections // NZ
    topk = route_ids.shape[4]
    window = spread // GROUP
    rows = spread * CAP
    slots = spread // 2 * CAP * window
    count = spread // 2 * tokens
    lanes = FLOWS * 2 * window * CAP
    vmem = pl.BlockSpec(memory_space=pltpu.VMEM)
    hbm = pl.BlockSpec(memory_space=pl.ANY)
    dma = pltpu.SemaphoreType.DMA
    return pl.pallas_call(
        kernel,
        out_shape=jax.ShapeDtypeStruct((2, 2, tokens, chunk), BF16),
        in_specs=[hbm, hbm, hbm, hbm, hbm, hbm, hbm],
        out_specs=vmem,
        scratch_shapes=[
            pltpu.VMEM((width, hid), BF16),
            pltpu.VMEM((width, hid), BF16),
            pltpu.VMEM((hid, width), BF16),
            pltpu.VMEM((2, 2, tokens, chunk * NY), BF16),
            pltpu.VMEM((2, NY, tokens, WIDE), BF16),
            pltpu.VMEM((sections, WIDE), F32),
            pltpu.VMEM((FLOWS, sections, rows, WIDE), BF16),
            pltpu.VMEM((FLOWS, nx, NY // 2, rows, WIDE), BF16),
            pltpu.VMEM((nx, rows, chunk * NY), BF16),
            pltpu.VMEM((rows, hid), BF16),
            pltpu.VMEM((nx, spread, tokens, WIDE), BF16),
            pltpu.VMEM((nx, spread, tokens, WIDE), BF16),
            pltpu.VMEM((nx + 1, window, rows, WIDE), BF16),
            pltpu.VMEM((nx, window, rows, WIDE), BF16),
            pltpu.VMEM((FLOWS, tokens, WIDE), BF16),
            pltpu.VMEM((1, 1, lanes), F32),
            pltpu.VMEM((2 * nx + 1, spread, 1, lanes), F32),
            pltpu.VMEM((2, count, slots), BF16),
            pltpu.VMEM((2, count, slots), BF16),
            pltpu.VMEM((2, slots, count), BF16),
            pltpu.SemaphoreType.REGULAR,
            pltpu.VMEM((1, width), F32),
            pltpu.VMEM((2, 2, 1, topk, tokens), jnp.int32),
            pltpu.VMEM((2, 2, 1, topk, tokens), F32),
            dma((3,)),
            pltpu.VMEM((FLOWS, nx, NY // 2, rows, WIDE), BF16),
            pltpu.VMEM((FLOWS, nx, NY // 2, rows, WIDE), BF16),
            dma((FLOWS,)),
            dma((FLOWS, sections)),
            dma((FLOWS,)),
            dma((3,)),
            dma,
            dma((2, NY)),
            dma,
            dma((FLOWS, sections)),
            dma((FLOWS,)),
            dma((nx + 1,)),
            dma((nx,)),
            dma((nx,)),
            dma((nx,)),
            dma,
            dma((FLOWS,)),
            dma,
            dma((2 * nx + 1,)),
        ],
        compiler_params=pltpu.CompilerParams(
            has_side_effects=True, vmem_limit_bytes=60 * 2**20
        ),
        cost_estimate=pl.CostEstimate(
            flops=2 * FLOWS * rows * width * hid * 3,
            bytes_accessed=width * hid * 6,
            transcendentals=0,
        ),
        name="relay",
    )(
        entering, norm_gain, w_gate, w_up, w_down,
        jnp.swapaxes(route_ids, 3, 4), jnp.swapaxes(route_scores, 3, 4),
    )


def solution(mesh):
    return jax.shard_map(
        on_device,
        mesh=mesh,
        in_specs=(
            P(None, None, "expert", None),
            P("section", None),
            P("section", None, "expert"),
            P("section", None, "expert"),
            P("section", "expert", None),
            P(None, None, "section", "expert", None),
            P(None, None, "section", "expert", None),
        ),
        out_specs=P(None, None, "expert", "section"),
        check_vma=False,
    )
```

```python
import jax
import jax.numpy as jnp
from jax import lax
from jax.experimental import pallas as pl
from jax.experimental.pallas import tpu as pltpu
from jax.sharding import PartitionSpec as P

MESH = pl.DeviceIdType.MESH
BF16, F32 = jnp.bfloat16, jnp.float32

GROUP = 2
CAP = 2
FLOWS = 4
WIDE = 256
NZ = 4
NY = 4
FAR = 9

norm_eps = 1e-06
route_scale = 2.5


def home_of(flow, x, y):
    return lax.rem(x + y + flow // 2, 2) * (2 * NY) + y * 2 + flow % 2


def iota(shape, dim):
    return lax.broadcasted_iota(jnp.int32, shape, dim)


def kernel(
    entering, gain_h, wg_h, wu_h, wd_h, ids_h, scores_h, out,
    wg, wu, wd, raw, xin, gain, ein, eout, part, act,
    hx, hnew, hrows, hparts, fin, tabrow, tab, chi, clo, place,
    picked, mhi, mlo, norm_gain, ids, scores, gain_sem, eswap, pin, swap_send, pin_sem, pass_send,
    w_sem, raw_sem, init_send, init_recv, ein_sem, eout_sem, rows_sem, parts_sem,
    move_send, move_recv, fin_send, fin_recv, tab_send, tab_recv,
):
    sections = lax.axis_size("section")
    spread = lax.axis_size("expert")
    window = spread // GROUP
    nx = sections // NZ
    sec, exp = lax.axis_index("section"), lax.axis_index("expert")
    my_x, my_z = sec // NZ, lax.rem(sec, NZ)
    my_y = lax.rem(exp // 2, NY)
    tokens = ids.shape[4]
    width = wg_h.shape[1]
    chunk = width // sections
    block = chunk * NY
    hid = wg_h.shape[2]
    last = sections - 1
    half = spread // 2
    slots = half * CAP * window
    count = half * tokens

    flow = lax.rem(exp // (2 * NY) + my_x + my_y, 2) * 2 + lax.rem(exp, 2)
    way = flow // 2
    my_chunk = my_x * NY + my_y
    starts = my_z == way * (NZ - 1)
    ends = my_z == (1 - way) * (NZ - 1)
    first_visit = way * (nx - 1)

    def send(src, dst, send_sem, recv_sem, section, device):
        here = (section == sec) & (device == exp)

        @pl.when(here)
        def _():
            pltpu.make_async_copy(src, dst, recv_sem).start()

        @pl.when(jnp.logical_not(here))
        def _():
            pltpu.make_async_remote_copy(
                src_ref=src, dst_ref=dst, send_sem=send_sem, recv_sem=recv_sem,
                device_id=(section, device), device_id_type=MESH,
            ).start()

    def sent(src, send_sem, section, device):
        @pl.when(jnp.logical_not((section == sec) & (device == exp)))
        def _():
            pltpu.make_async_copy(src, src, send_sem).wait()

    def arrived(ref, sem):
        pltpu.make_async_copy(ref, ref, sem).wait()

    mine_in = entering.at[:, :, :, pl.ds(pl.multiple_of(my_x * block, 128), block)]
    fetch = pltpu.make_async_copy(mine_in, raw, raw_sem)
    small = [
        pltpu.make_async_copy(src, dst, gain_sem.at[k])
        for k, (src, dst) in enumerate(((ids_h, ids), (scores_h, scores), (gain_h, norm_gain)))
    ]
    for copy in small:
        copy.start()
    fetch.start()
    weights = [
        pltpu.make_async_copy(src.at[0], dst, w_sem.at[k])
        for k, (src, dst) in enumerate(((wg_h, wg), (wu_h, wu), (wd_h, wd)))
    ]

    for copy in weights:
        copy.start()
    for copy in small:
        copy.wait()

    lanes = FLOWS * 2 * window * CAP
    lane = iota((1, lanes), 1)
    lane_expert = lax.rem(lane // CAP, window)
    lane_slot = lax.rem(lane, CAP).astype(F32)
    lane_kind = lax.rem(lane // (CAP * window), 2)
    lane_flow = lane // (2 * CAP * window)
    earlier = (iota((tokens, tokens), 0) > iota((tokens, tokens), 1)).astype(BF16)
    number = iota((tokens, lanes), 0).astype(F32) + 1.0
    table = jnp.zeros((1, lanes), F32)
    for f in range(FLOWS):
        chosen = ids[f // 2, f % 2, 0].T
        score = scores[f // 2, f % 2, 0].T
        weight = route_scale * score / jnp.sum(score, axis=1, keepdims=True)
        hit = jnp.zeros((tokens, lanes), F32)
        share = jnp.zeros((tokens, lanes), F32)
        for k in range(chosen.shape[1]):
            same = chosen[:, k : k + 1] == lane_expert
            hit += jnp.where(same, 1.0, 0.0)
            share += jnp.where(same, weight[:, k : k + 1], 0.0)
        before = jnp.dot(earlier, hit.astype(BF16), preferred_element_type=F32)
        held = jnp.where(before == lane_slot, hit, 0.0)
        value = jnp.where(lane_kind == 0, number, share)
        row = jnp.sum(held * value, axis=0, keepdims=True) - jnp.where(lane_kind == 0, 1.0, 0.0)
        table += jnp.where(lane_flow == f, row, 0.0)
    tabrow[0] = table

    def tables(deliver, first):
        for f in range(FLOWS):
            d = f // 2
            prior = sec + (2 * d - 1)

            def one(c, unused):
                x, y = c // NY, lax.rem(c, NY)
                device = home_of(f, x, y)

                if first:
                    deliver(2 * nx, x * NZ + my_z, device)
                    return unused

                @pl.when((prior >= 0) & (prior <= last))
                def _():
                    deliver(nx + prior // NZ, x * NZ + lax.rem(prior, NZ), device)

                deliver(my_x, x * NZ + my_z, device)
                return unused

            if first:

                @pl.when(sec == d * last)
                def _():
                    lax.fori_loop(0, sections, one, 0)

            else:
                lax.fori_loop(0, sections, one, 0)

    def deliver_table(use, section, device):
        send(tabrow.at[0], tab.at[use, exp], tab_send, tab_recv.at[use], section, device)

    def drain_table(use, section, device):
        sent(tabrow.at[0], tab_send, section, device)

    tables(deliver_table, True)
    fetch.wait()

    def enter(act_on):
        for f in range(FLOWS):
            d, m = f // 2, f % 2

            @pl.when(my_z == d * (NZ - 1))
            def _():
                for y in range(NY):
                    act_on(f, d, m, y, home_of(f, my_x, y))

    def send_entering(f, d, m, y, device):
        xin[m, y] = jnp.zeros((tokens, WIDE), BF16)
        xin[m, y, :, :chunk] = raw[d, m, :, y * chunk : (y + 1) * chunk]
        send(xin.at[m, y], hx.at[d * (nx - 1), exp], init_send.at[m, y], init_recv, sec, device)

    def sent_entering(f, d, m, y, device):
        sent(xin.at[m, y], init_send.at[m, y], sec, device)

    enter(send_entering)
    spot = iota((1, slots), 1)
    spot_lane = (spot // (half * CAP)) * CAP + lax.rem(spot, CAP)
    spot_block = lax.rem(spot // CAP, half)

    def pick(kind):
        return (iota((lanes, slots), 0) == (flow * 2 + kind) * (window * CAP) + spot_lane).astype(F32)

    def rows_of(use, kind):
        got = jnp.concatenate([tab[use, b] for b in range(spread)], axis=0)
        wide = jnp.dot(got, pick(kind), precision=lax.Precision.HIGHEST, preferred_element_type=F32)
        own = lax.rem(iota((spread, slots), 0), half) == spot_block
        kept = jnp.where(own, wide, 0.0)
        return [jnp.sum(kept[g * half : (g + 1) * half], axis=0, keepdims=True) for g in range(2)]

    def prepare_sums(use):
        arrived(tab.at[use], tab_recv.at[use])
        toks, shares = rows_of(use, 0), rows_of(use, 1)
        for g in range(2):
            tok = jnp.where(toks[g] < -0.5, -1.0, toks[g] + (spot_block * tokens).astype(F32))
            comb = jnp.where(iota((count, slots), 0).astype(F32) == tok, shares[g], 0.0)
            high = comb.astype(BF16)
            low = (comb - high.astype(F32)).astype(BF16)
            chi[g] = high
            clo[g] = low

    def prepare_rows(use):
        arrived(tab.at[use], tab_recv.at[use])
        toks = rows_of(use, 0)
        for g in range(2):
            tok = jnp.where(toks[g] < -0.5, -1.0, toks[g] + (spot_block * tokens).astype(F32))
            col = jnp.broadcast_to(tok, (slots, slots)).T[:, :1]
            place[g] = (iota((slots, count), 1).astype(F32) == col).astype(BF16)

    def pick_rows(k):
        for g in range(2):
            x = hx[k, g * half : (g + 1) * half].reshape(count, WIDE)
            picked[g] = jnp.dot(place[g], x, preferred_element_type=F32)

    def far_from(x, y):
        dx = lax.rem(my_x - x + nx, nx)
        dy = lax.rem(my_y - y + NY, NY)
        return jnp.minimum(dx, nx - dx) + jnp.minimum(dy, NY - dy) >= FAR

    def rows_to(k, layer, act_on):
        def one(i, unused):
            e = lax.rem(i + (my_y + 1) * 2, 2 * NY) + (i // (2 * NY)) * 2 * NY
            takes = lax.rem(e, 2) == lax.rem(my_y, 2)

            @pl.when(takes | far_from(layer // NZ, lax.rem(e // 2, NY)))
            def _():
                act_on(
                    hrows.at[k, e // GROUP], ein.at[flow, my_chunk],
                    rows_sem.at[k], ein_sem.at[flow, my_chunk], layer, e,
                )

            return unused

        lax.fori_loop(0, spread, one, 0)

    def drain_rows(src, dst, send_sem, recv_sem, section, device):
        sent(src, send_sem, section, device)

    def sums(k, g, high, low):
        got = hparts[k, :, g * half * CAP : (g + 1) * half * CAP, :].reshape(slots, WIDE)
        added = jnp.dot(high, got, preferred_element_type=F32)
        return added + jnp.dot(low, got, preferred_element_type=F32)

    def dispatch(k, layer, added):
        for g in range(2):
            rows = picked[g]
            if added:
                rows += sums(added[0], g, mhi[g], mlo[g])
            rows = rows.astype(BF16)
            hrows[k, :, g * half * CAP : (g + 1) * half * CAP, :] = rows.reshape(
                window, half * CAP, WIDE
            )

        rows_to(k, layer, send)


    @pl.when(starts)
    def _():
        prepare_rows(2 * nx)
        arrived(hx.at[first_visit], init_recv)
        pick_rows(first_visit)
        dispatch(nx, way * last, ())

    tables(deliver_table, False)
    eout[...] = jnp.zeros_like(eout)
    eswap[...] = jnp.zeros_like(eswap)
    for c in range(sections):
        gain[c : c + 1, :] = jnp.zeros((1, WIDE), F32)
        gain[c : c + 1, :chunk] = norm_gain[:, c * chunk : (c + 1) * chunk]
    tables(drain_table, True)
    tables(drain_table, False)
    enter(sent_entering)

    around = sorted(
        ((dx, dy) for dx in range(nx) for dy in range(NY // 2)),
        key=lambda o: (min(o[0], nx - o[0]) + 2 * o[1], o),
    )
    core = lax.rem(exp, 2)
    sibling = exp + 1 - 2 * core
    columns = [dx for dx in (1, 2, 3, 0) if dx < nx]

    def expert_phase(f):
        gate = jnp.zeros((spread * CAP, hid), F32)
        up = jnp.zeros((spread * CAP, hid), F32)
        square = jnp.zeros((spread * CAP, WIDE), F32)
        for passes in (True, False):
            for dx, half_dy in around:
                odd = lax.rem(my_y + core, 2) if passes else lax.rem(my_y + core + 1, 2)
                y = lax.rem(my_y + 2 * half_dy + odd, NY)
                c = lax.rem(my_x + dx, nx) * NY + y
                arrived(ein.at[f, c], ein_sem.at[f, c])
                if passes:

                    @pl.when(jnp.logical_not(far_from(lax.rem(my_x + dx, nx), y)))
                    def _():
                        pltpu.make_async_remote_copy(
                            src_ref=ein.at[f, c], dst_ref=ein.at[f, c],
                            send_sem=pass_send.at[f], recv_sem=ein_sem.at[f, c],
                            device_id=(sec, sibling), device_id_type=MESH,
                        ).start()

                x = ein[f, c].astype(F32)
                square += x * x
                h = (x * gain[pl.ds(c, 1), :]).astype(BF16)[:, :chunk]
                rows = pl.ds(pl.multiple_of(c * chunk, 32), chunk)
                gate += jnp.dot(h, wg[rows, :], preferred_element_type=F32)
                up += jnp.dot(h, wu[rows, :], preferred_element_type=F32)
        scale = lax.rsqrt(jnp.sum(square, axis=1, keepdims=True) / width + norm_eps)
        gate = gate * scale
        up = up * scale
        act[...] = (gate / (1.0 + jnp.exp(-gate)) * up).astype(BF16)
        for n, dx in enumerate(columns):
            x = lax.rem(my_x + dx, nx)
            cols = pl.ds(pl.multiple_of(x * block, 128), block)
            part[n] = jnp.dot(act[...], wd[:, cols], preferred_element_type=F32).astype(BF16)
            for y in range(NY):

                @pl.when(core != y % 2)
                def _():
                    c = x * NY + y
                    eswap[f, x, y // 2, :, :chunk] = part[n, :, y * chunk : (y + 1) * chunk]
                    pltpu.make_async_remote_copy(
                        src_ref=eswap.at[f, x, y // 2], dst_ref=pin.at[f, x, y // 2],
                        send_sem=swap_send.at[f], recv_sem=pin_sem.at[f, c],
                        device_id=(sec, sibling), device_id_type=MESH,
                    ).start()

        for n, dx in enumerate(columns):
            x = lax.rem(my_x + dx, nx)
            for y in range(NY):

                @pl.when(core == y % 2)
                def _():
                    c = x * NY + y
                    arrived(pin.at[f, x, y // 2], pin_sem.at[f, c])
                    own = part[n, :, y * chunk : (y + 1) * chunk].astype(F32)
                    other = pin[f, x, y // 2, :, :chunk].astype(F32)
                    eout[f, x, y // 2, :, :chunk] = (own + other).astype(BF16)
                    send(
                        eout.at[f, x, y // 2], hparts.at[my_x, exp // GROUP], eout_sem.at[f],
                        parts_sem.at[my_x], x * NZ + my_z, home_of(f, x, y),
                    )

    def home_phase(k, layer):
        following = layer + 1 - 2 * way
        onward = (following >= 0) & (following <= last)
        prepare_sums(k)

        @pl.when(onward)
        def _():
            prepare_rows(nx + k)
            for g in range(2):
                mhi[g] = jnp.dot(place[g], chi[g], preferred_element_type=F32).astype(BF16)
                mlo[g] = jnp.dot(place[g], clo[g], preferred_element_type=F32).astype(BF16)

        @pl.when(jnp.logical_not(starts & (k == first_visit)))
        def _():
            arrived(hx.at[k], move_recv.at[k])

        @pl.when(onward)
        def _():
            pick_rows(k)

        arrived(hparts.at[k], parts_sem.at[k])

        @pl.when(onward)
        def _():
            dispatch(k, following, (k,))

        for g in range(2):
            old = hx[k, g * half : (g + 1) * half].reshape(count, WIDE)
            new = (old.astype(F32) + sums(k, g, chi[g], clo[g])).astype(BF16)
            hnew[k, g * half : (g + 1) * half] = new.reshape(half, tokens, WIDE)

        @pl.when(onward)
        def _():
            pltpu.make_async_remote_copy(
                src_ref=hnew.at[k], dst_ref=hx.at[following // NZ],
                send_sem=move_send.at[k], recv_sem=move_recv.at[following // NZ],
                device_id=(my_x * NZ + lax.rem(following, NZ), exp), device_id_type=MESH,
            ).start()

        @pl.when(jnp.logical_not(onward))
        def _():
            def one(b, unused):
                send(hnew.at[k, b], fin.at[flow], fin_send, fin_recv.at[flow], my_chunk, b)
                return unused

            lax.fori_loop(0, spread, one, 0)

    def step(t, unused):
        @pl.when(t == jnp.minimum(sec, last - sec))
        def _():
            for copy in weights:
                copy.wait()

        def direction(d, unused):
            @pl.when(t == jnp.where(d == 0, sec, last - sec))
            def _():
                def micro(m, unused):
                    expert_phase(d * 2 + m)
                    return unused

                lax.fori_loop(0, 2, micro, 0)

            return unused

        lax.fori_loop(0, 2, direction, 0)
        layer = jnp.where(way == 0, t, last - t)

        @pl.when(lax.rem(layer, NZ) == my_z)
        def _():
            home_phase(layer // NZ, layer)

        return unused

    lax.fori_loop(0, sections, step, 0)

    for f in range(FLOWS):
        arrived(eswap.at[f], swap_send.at[f])
        inner = [
            (dx, dy) for dx in range(nx) for dy in range(NY)
            if min(dx, nx - dx) + min(dy, NY - dy) < FAR
        ]
        for parity in range(2):
            passed = sum(1 for _, dy in inner if dy % 2 == parity)

            @pl.when(lax.rem(my_y + core, 2) == parity)
            def _():
                arrived(ein.at[f, :passed], pass_send.at[f])

        own = (f == flow) & (core == lax.rem(my_y, 2))

        @pl.when(own)
        def _():
            arrived(ein.at[f, 1 : sections // 2], eout_sem.at[f])

        @pl.when(jnp.logical_not(own))
        def _():
            arrived(ein.at[f, : sections // 2], eout_sem.at[f])

    for k in range(nx):
        final = ends & (k == (1 - way) * (nx - 1))

        @pl.when(jnp.logical_not(final))
        def _():
            rows_to(k, NZ * k + my_z + 1 - 2 * way, drain_rows)
            arrived(hnew.at[k], move_send.at[k])

        @pl.when(final)
        def _():
            lax.fori_loop(
                0, spread, lambda b, unused: (sent(hnew.at[k, 0], fin_send, my_chunk, b), unused)[1], 0
            )

    @pl.when(starts)
    def _():
        rows_to(nx, way * last, drain_rows)

    for f in range(FLOWS):
        arrived(fin.at[f], fin_recv.at[f])
        out[f // 2, f % 2] = fin[f][:, :chunk]


def on_device(entering, norm_gain, w_gate, w_up, w_down, route_ids, route_scores):
    sections = lax.axis_size("section")
    spread = lax.axis_size("expert")
    tokens, width = entering.shape[2:]
    chunk = width // sections
    hid = w_gate.shape[2]
    nx = sections // NZ
    topk = route_ids.shape[4]
    window = spread // GROUP
    rows = spread * CAP
    slots = spread // 2 * CAP * window
    count = spread // 2 * tokens
    lanes = FLOWS * 2 * window * CAP
    vmem = pl.BlockSpec(memory_space=pltpu.VMEM)
    hbm = pl.BlockSpec(memory_space=pl.ANY)
    dma = pltpu.SemaphoreType.DMA
    return pl.pallas_call(
        kernel,
        out_shape=jax.ShapeDtypeStruct((2, 2, tokens, chunk), BF16),
        in_specs=[hbm, hbm, hbm, hbm, hbm, hbm, hbm],
        out_specs=vmem,
        scratch_shapes=[
            pltpu.VMEM((width, hid), BF16),
            pltpu.VMEM((width, hid), BF16),
            pltpu.VMEM((hid, width), BF16),
            pltpu.VMEM((2, 2, tokens, chunk * NY), BF16),
            pltpu.VMEM((2, NY, tokens, WIDE), BF16),
            pltpu.VMEM((sections, WIDE), F32),
            pltpu.VMEM((FLOWS, sections, rows, WIDE), BF16),
            pltpu.VMEM((FLOWS, nx, NY // 2, rows, WIDE), BF16),
            pltpu.VMEM((nx, rows, chunk * NY), BF16),
            pltpu.VMEM((rows, hid), BF16),
            pltpu.VMEM((nx, spread, tokens, WIDE), BF16),
            pltpu.VMEM((nx, spread, tokens, WIDE), BF16),
            pltpu.VMEM((nx + 1, window, rows, WIDE), BF16),
            pltpu.VMEM((nx, window, rows, WIDE), BF16),
            pltpu.VMEM((FLOWS, tokens, WIDE), BF16),
            pltpu.VMEM((1, 1, lanes), F32),
            pltpu.VMEM((2 * nx + 1, spread, 1, lanes), F32),
            pltpu.VMEM((2, count, slots), BF16),
            pltpu.VMEM((2, count, slots), BF16),
            pltpu.VMEM((2, slots, count), BF16),
            pltpu.VMEM((2, slots, WIDE), F32),
            pltpu.VMEM((2, slots, slots), BF16),
            pltpu.VMEM((2, slots, slots), BF16),
            pltpu.VMEM((1, width), F32),
            pltpu.VMEM((2, 2, 1, topk, tokens), jnp.int32),
            pltpu.VMEM((2, 2, 1, topk, tokens), F32),
            dma((3,)),
            pltpu.VMEM((FLOWS, nx, NY // 2, rows, WIDE), BF16),
            pltpu.VMEM((FLOWS, nx, NY // 2, rows, WIDE), BF16),
            dma((FLOWS,)),
            dma((FLOWS, sections)),
            dma((FLOWS,)),
            dma((3,)),
            dma,
            dma((2, NY)),
            dma,
            dma((FLOWS, sections)),
            dma((FLOWS,)),
            dma((nx + 1,)),
            dma((nx,)),
            dma((nx,)),
            dma((nx,)),
            dma,
            dma((FLOWS,)),
            dma,
            dma((2 * nx + 1,)),
        ],
        compiler_params=pltpu.CompilerParams(
            has_side_effects=True, vmem_limit_bytes=60 * 2**20
        ),
        cost_estimate=pl.CostEstimate(
            flops=2 * FLOWS * rows * width * hid * 3,
            bytes_accessed=width * hid * 6,
            transcendentals=0,
        ),
        name="relay",
    )(
        entering, norm_gain, w_gate, w_up, w_down,
        jnp.swapaxes(route_ids, 3, 4), jnp.swapaxes(route_scores, 3, 4),
    )


def solution(mesh):
    return jax.shard_map(
        on_device,
        mesh=mesh,
        in_specs=(
            P(None, None, "expert", None),
            P("section", None),
            P("section", None, "expert"),
            P("section", None, "expert"),
            P("section", "expert", None),
            P(None, None, "section", "expert", None),
            P(None, None, "section", "expert", None),
        ),
        out_specs=P(None, None, "expert", "section"),
        check_vma=False,
    )
```

```python
import jax
import jax.numpy as jnp
from jax import lax
from jax.experimental import pallas as pl
from jax.experimental.pallas import tpu as pltpu
from jax.sharding import PartitionSpec as P

MESH = pl.DeviceIdType.MESH
BF16, F32 = jnp.bfloat16, jnp.float32

GROUP = 2
CAP = 2
FLOWS = 4
WIDE = 256
NZ = 4
NY = 4
FAR = 9

norm_eps = 1e-06
route_scale = 2.5


def home_of(flow, x, y):
    return lax.rem(x + y + flow // 2, 2) * (2 * NY) + y * 2 + flow % 2


def iota(shape, dim):
    return lax.broadcasted_iota(jnp.int32, shape, dim)


def kernel(
    entering, gain_h, wg_h, wu_h, wd_h, ids_h, scores_h, out,
    wg, wu, wd, raw, xin, gain, ein, eout, part, act,
    hx, hnew, hrows, hparts, fin, tabrow, tab, chi, clo, place,
    picked, mhi, mlo, norm_gain, ids, scores, gain_sem, eswap, pin, swap_send, pin_sem, pass_send,
    w_sem, raw_sem, init_send, init_recv, ein_sem, eout_sem, rows_sem, parts_sem,
    move_send, move_recv, fin_send, fin_recv, tab_send, tab_recv,
):
    sections = lax.axis_size("section")
    spread = lax.axis_size("expert")
    window = spread // GROUP
    nx = sections // NZ
    sec, exp = lax.axis_index("section"), lax.axis_index("expert")
    my_x, my_z = sec // NZ, lax.rem(sec, NZ)
    my_y = lax.rem(exp // 2, NY)
    tokens = ids.shape[4]
    width = wg_h.shape[1]
    chunk = width // sections
    block = chunk * NY
    hid = wg_h.shape[2]
    last = sections - 1
    half = spread // 2
    slots = half * CAP * window
    count = half * tokens

    flow = lax.rem(exp // (2 * NY) + my_x + my_y, 2) * 2 + lax.rem(exp, 2)
    way = flow // 2
    my_chunk = my_x * NY + my_y
    starts = my_z == way * (NZ - 1)
    ends = my_z == (1 - way) * (NZ - 1)
    first_visit = way * (nx - 1)

    def send(src, dst, send_sem, recv_sem, section, device):
        here = (section == sec) & (device == exp)

        @pl.when(here)
        def _():
            pltpu.make_async_copy(src, dst, recv_sem).start()

        @pl.when(jnp.logical_not(here))
        def _():
            pltpu.make_async_remote_copy(
                src_ref=src, dst_ref=dst, send_sem=send_sem, recv_sem=recv_sem,
                device_id=(section, device), device_id_type=MESH,
            ).start()

    def sent(src, send_sem, section, device):
        @pl.when(jnp.logical_not((section == sec) & (device == exp)))
        def _():
            pltpu.make_async_copy(src, src, send_sem).wait()

    def arrived(ref, sem):
        pltpu.make_async_copy(ref, ref, sem).wait()

    mine_in = entering.at[:, :, :, pl.ds(pl.multiple_of(my_x * block, 128), block)]
    fetch = pltpu.make_async_copy(mine_in, raw, raw_sem)
    small = [
        pltpu.make_async_copy(src, dst, gain_sem.at[k])
        for k, (src, dst) in enumerate(((ids_h, ids), (scores_h, scores), (gain_h, norm_gain)))
    ]
    for copy in small:
        copy.start()
    fetch.start()
    weights = [
        pltpu.make_async_copy(src.at[0], dst, w_sem.at[k])
        for k, (src, dst) in enumerate(((wg_h, wg), (wu_h, wu), (wd_h, wd)))
    ]

    for copy in weights:
        copy.start()
    for copy in small:
        copy.wait()

    lanes = FLOWS * 2 * window * CAP
    lane = iota((1, lanes), 1)
    lane_expert = lax.rem(lane // CAP, window)
    lane_slot = lax.rem(lane, CAP).astype(F32)
    lane_kind = lax.rem(lane // (CAP * window), 2)
    lane_flow = lane // (2 * CAP * window)
    earlier = (iota((tokens, tokens), 0) > iota((tokens, tokens), 1)).astype(BF16)
    number = iota((tokens, lanes), 0).astype(F32) + 1.0
    table = jnp.zeros((1, lanes), F32)
    for f in range(FLOWS):
        chosen = ids[f // 2, f % 2, 0].T
        score = scores[f // 2, f % 2, 0].T
        weight = route_scale * score / jnp.sum(score, axis=1, keepdims=True)
        hit = jnp.zeros((tokens, lanes), F32)
        share = jnp.zeros((tokens, lanes), F32)
        for k in range(chosen.shape[1]):
            same = chosen[:, k : k + 1] == lane_expert
            hit += jnp.where(same, 1.0, 0.0)
            share += jnp.where(same, weight[:, k : k + 1], 0.0)
        before = jnp.dot(earlier, hit.astype(BF16), preferred_element_type=F32)
        held = jnp.where(before == lane_slot, hit, 0.0)
        value = jnp.where(lane_kind == 0, number, share)
        row = jnp.sum(held * value, axis=0, keepdims=True) - jnp.where(lane_kind == 0, 1.0, 0.0)
        table += jnp.where(lane_flow == f, row, 0.0)
    tabrow[0] = table

    def tables(deliver, first):
        for f in range(FLOWS):
            d = f // 2
            prior = sec + (2 * d - 1)

            def one(c, unused):
                x, y = c // NY, lax.rem(c, NY)
                device = home_of(f, x, y)

                if first:
                    deliver(2 * nx, x * NZ + my_z, device)
                    return unused

                @pl.when((prior >= 0) & (prior <= last))
                def _():
                    deliver(nx + prior // NZ, x * NZ + lax.rem(prior, NZ), device)

                deliver(my_x, x * NZ + my_z, device)
                return unused

            if first:

                @pl.when(sec == d * last)
                def _():
                    lax.fori_loop(0, sections, one, 0)

            else:
                lax.fori_loop(0, sections, one, 0)

    def deliver_table(use, section, device):
        send(tabrow.at[0], tab.at[use, exp], tab_send, tab_recv.at[use], section, device)

    def drain_table(use, section, device):
        sent(tabrow.at[0], tab_send, section, device)

    tables(deliver_table, True)
    fetch.wait()

    def enter(act_on):
        for f in range(FLOWS):
            d, m = f // 2, f % 2

            @pl.when(my_z == d * (NZ - 1))
            def _():
                for y in range(NY):
                    act_on(f, d, m, y, home_of(f, my_x, y))

    def send_entering(f, d, m, y, device):
        xin[m, y] = jnp.zeros((tokens, WIDE), BF16)
        xin[m, y, :, :chunk] = raw[d, m, :, y * chunk : (y + 1) * chunk]
        send(xin.at[m, y], hx.at[d * (nx - 1), exp], init_send.at[m, y], init_recv, sec, device)

    def sent_entering(f, d, m, y, device):
        sent(xin.at[m, y], init_send.at[m, y], sec, device)

    enter(send_entering)
    spot = iota((1, slots), 1)
    spot_lane = (spot // (half * CAP)) * CAP + lax.rem(spot, CAP)
    spot_block = lax.rem(spot // CAP, half)

    def pick(kind):
        return (iota((lanes, slots), 0) == (flow * 2 + kind) * (window * CAP) + spot_lane).astype(F32)

    def rows_of(use, kind):
        got = jnp.concatenate([tab[use, b] for b in range(spread)], axis=0)
        wide = jnp.dot(got, pick(kind), precision=lax.Precision.HIGHEST, preferred_element_type=F32)
        own = lax.rem(iota((spread, slots), 0), half) == spot_block
        kept = jnp.where(own, wide, 0.0)
        return [jnp.sum(kept[g * half : (g + 1) * half], axis=0, keepdims=True) for g in range(2)]

    def prepare_sums(use):
        arrived(tab.at[use], tab_recv.at[use])
        toks, shares = rows_of(use, 0), rows_of(use, 1)
        for g in range(2):
            tok = jnp.where(toks[g] < -0.5, -1.0, toks[g] + (spot_block * tokens).astype(F32))
            comb = jnp.where(iota((count, slots), 0).astype(F32) == tok, shares[g], 0.0)
            high = comb.astype(BF16)
            low = (comb - high.astype(F32)).astype(BF16)
            chi[g] = high
            clo[g] = low

    def prepare_rows(use):
        arrived(tab.at[use], tab_recv.at[use])
        toks = rows_of(use, 0)
        for g in range(2):
            tok = jnp.where(toks[g] < -0.5, -1.0, toks[g] + (spot_block * tokens).astype(F32))
            col = jnp.broadcast_to(tok, (slots, slots)).T[:, :1]
            place[g] = (iota((slots, count), 1).astype(F32) == col).astype(BF16)

    def pick_rows(k):
        for g in range(2):
            x = hx[k, g * half : (g + 1) * half].reshape(count, WIDE)
            picked[g] = jnp.dot(place[g], x, preferred_element_type=F32)

    def far_from(x, y):
        dx = lax.rem(my_x - x + nx, nx)
        dy = lax.rem(my_y - y + NY, NY)
        return jnp.minimum(dx, nx - dx) + jnp.minimum(dy, NY - dy) >= FAR

    def rows_to(k, layer, act_on):
        def one(i, unused):
            e = lax.rem(i + (my_y + 1) * 2, 2 * NY) + lax.rem(i // (2 * NY) + 1 + way, 2) * 2 * NY
            takes = lax.rem(e, 2) == lax.rem(my_y, 2)

            @pl.when(takes | far_from(layer // NZ, lax.rem(e // 2, NY)))
            def _():
                act_on(
                    hrows.at[k, e // GROUP], ein.at[flow, my_chunk],
                    rows_sem.at[k], ein_sem.at[flow, my_chunk], layer, e,
                )

            return unused

        lax.fori_loop(0, spread, one, 0)

    def drain_rows(src, dst, send_sem, recv_sem, section, device):
        sent(src, send_sem, section, device)

    def sums(k, g, high, low):
        got = hparts[k, :, g * half * CAP : (g + 1) * half * CAP, :].reshape(slots, WIDE)
        added = jnp.dot(high, got, preferred_element_type=F32)
        return added + jnp.dot(low, got, preferred_element_type=F32)

    def dispatch(k, layer, added):
        for g in range(2):
            rows = picked[g]
            if added:
                rows += sums(added[0], g, mhi[g], mlo[g])
            rows = rows.astype(BF16)
            hrows[k, :, g * half * CAP : (g + 1) * half * CAP, :] = rows.reshape(
                window, half * CAP, WIDE
            )

        rows_to(k, layer, send)


    @pl.when(starts)
    def _():
        prepare_rows(2 * nx)
        arrived(hx.at[first_visit], init_recv)
        pick_rows(first_visit)
        dispatch(nx, way * last, ())

    tables(deliver_table, False)
    eout[...] = jnp.zeros_like(eout)
    eswap[...] = jnp.zeros_like(eswap)
    for c in range(sections):
        gain[c : c + 1, :] = jnp.zeros((1, WIDE), F32)
        gain[c : c + 1, :chunk] = norm_gain[:, c * chunk : (c + 1) * chunk]
    tables(drain_table, True)
    tables(drain_table, False)
    enter(sent_entering)

    around = sorted(
        ((dx, dy) for dx in range(nx) for dy in range(NY // 2)),
        key=lambda o: (min(o[0], nx - o[0]) + 2 * o[1], o),
    )
    core = lax.rem(exp, 2)
    sibling = exp + 1 - 2 * core
    columns = [dx for dx in (1, 2, 3, 0) if dx < nx]

    def expert_phase(f):
        gate = jnp.zeros((spread * CAP, hid), F32)
        up = jnp.zeros((spread * CAP, hid), F32)
        square = jnp.zeros((spread * CAP, WIDE), F32)
        for passes in (True, False):
            for dx, half_dy in around:
                odd = lax.rem(my_y + core, 2) if passes else lax.rem(my_y + core + 1, 2)
                y = lax.rem(my_y + 2 * half_dy + odd, NY)
                c = lax.rem(my_x + dx, nx) * NY + y
                arrived(ein.at[f, c], ein_sem.at[f, c])
                if passes:

                    @pl.when(jnp.logical_not(far_from(lax.rem(my_x + dx, nx), y)))
                    def _():
                        pltpu.make_async_remote_copy(
                            src_ref=ein.at[f, c], dst_ref=ein.at[f, c],
                            send_sem=pass_send.at[f], recv_sem=ein_sem.at[f, c],
                            device_id=(sec, sibling), device_id_type=MESH,
                        ).start()

                x = ein[f, c].astype(F32)
                square += x * x
                h = (x * gain[pl.ds(c, 1), :]).astype(BF16)[:, :chunk]
                rows = pl.ds(pl.multiple_of(c * chunk, 32), chunk)
                gate += jnp.dot(h, wg[rows, :], preferred_element_type=F32)
                up += jnp.dot(h, wu[rows, :], preferred_element_type=F32)
        scale = lax.rsqrt(jnp.sum(square, axis=1, keepdims=True) / width + norm_eps)
        gate = gate * scale
        up = up * scale
        act[...] = (gate / (1.0 + jnp.exp(-gate)) * up).astype(BF16)
        for n, dx in enumerate(columns):
            x = lax.rem(my_x + dx, nx)
            cols = pl.ds(pl.multiple_of(x * block, 128), block)
            part[n] = jnp.dot(act[...], wd[:, cols], preferred_element_type=F32).astype(BF16)
            for y in range(NY):

                @pl.when(core != y % 2)
                def _():
                    c = x * NY + y
                    eswap[f, x, y // 2, :, :chunk] = part[n, :, y * chunk : (y + 1) * chunk]
                    pltpu.make_async_remote_copy(
                        src_ref=eswap.at[f, x, y // 2], dst_ref=pin.at[f, x, y // 2],
                        send_sem=swap_send.at[f], recv_sem=pin_sem.at[f, c],
                        device_id=(sec, sibling), device_id_type=MESH,
                    ).start()

        for n, dx in enumerate(columns):
            x = lax.rem(my_x + dx, nx)
            for y in range(NY):

                @pl.when(core == y % 2)
                def _():
                    c = x * NY + y
                    arrived(pin.at[f, x, y // 2], pin_sem.at[f, c])
                    own = part[n, :, y * chunk : (y + 1) * chunk].astype(F32)
                    other = pin[f, x, y // 2, :, :chunk].astype(F32)
                    eout[f, x, y // 2, :, :chunk] = (own + other).astype(BF16)
                    send(
                        eout.at[f, x, y // 2], hparts.at[my_x, exp // GROUP], eout_sem.at[f],
                        parts_sem.at[my_x], x * NZ + my_z, home_of(f, x, y),
                    )

    def home_phase(k, layer):
        following = layer + 1 - 2 * way
        onward = (following >= 0) & (following <= last)
        prepare_sums(k)

        @pl.when(onward)
        def _():
            prepare_rows(nx + k)
            for g in range(2):
                mhi[g] = jnp.dot(place[g], chi[g], preferred_element_type=F32).astype(BF16)
                mlo[g] = jnp.dot(place[g], clo[g], preferred_element_type=F32).astype(BF16)

        @pl.when(jnp.logical_not(starts & (k == first_visit)))
        def _():
            arrived(hx.at[k], move_recv.at[k])

        @pl.when(onward)
        def _():
            pick_rows(k)

        arrived(hparts.at[k], parts_sem.at[k])

        @pl.when(onward)
        def _():
            dispatch(k, following, (k,))

        for g in range(2):
            old = hx[k, g * half : (g + 1) * half].reshape(count, WIDE)
            new = (old.astype(F32) + sums(k, g, chi[g], clo[g])).astype(BF16)
            hnew[k, g * half : (g + 1) * half] = new.reshape(half, tokens, WIDE)

        @pl.when(onward)
        def _():
            pltpu.make_async_remote_copy(
                src_ref=hnew.at[k], dst_ref=hx.at[following // NZ],
                send_sem=move_send.at[k], recv_sem=move_recv.at[following // NZ],
                device_id=(my_x * NZ + lax.rem(following, NZ), exp), device_id_type=MESH,
            ).start()

        @pl.when(jnp.logical_not(onward))
        def _():
            def one(b, unused):
                send(hnew.at[k, b], fin.at[flow], fin_send, fin_recv.at[flow], my_chunk, b)
                return unused

            lax.fori_loop(0, spread, one, 0)

    def step(t, unused):
        @pl.when(t == jnp.minimum(sec, last - sec))
        def _():
            for copy in weights:
                copy.wait()

        def direction(d, unused):
            @pl.when(t == jnp.where(d == 0, sec, last - sec))
            def _():
                def micro(m, unused):
                    expert_phase(d * 2 + m)
                    return unused

                lax.fori_loop(0, 2, micro, 0)

            return unused

        lax.fori_loop(0, 2, direction, 0)
        layer = jnp.where(way == 0, t, last - t)

        @pl.when(lax.rem(layer, NZ) == my_z)
        def _():
            home_phase(layer // NZ, layer)

        return unused

    lax.fori_loop(0, sections, step, 0)

    for f in range(FLOWS):
        arrived(eswap.at[f], swap_send.at[f])
        inner = [
            (dx, dy) for dx in range(nx) for dy in range(NY)
            if min(dx, nx - dx) + min(dy, NY - dy) < FAR
        ]
        for parity in range(2):
            passed = sum(1 for _, dy in inner if dy % 2 == parity)

            @pl.when(lax.rem(my_y + core, 2) == parity)
            def _():
                arrived(ein.at[f, :passed], pass_send.at[f])

        own = (f == flow) & (core == lax.rem(my_y, 2))

        @pl.when(own)
        def _():
            arrived(ein.at[f, 1 : sections // 2], eout_sem.at[f])

        @pl.when(jnp.logical_not(own))
        def _():
            arrived(ein.at[f, : sections // 2], eout_sem.at[f])

    for k in range(nx):
        final = ends & (k == (1 - way) * (nx - 1))

        @pl.when(jnp.logical_not(final))
        def _():
            rows_to(k, NZ * k + my_z + 1 - 2 * way, drain_rows)
            arrived(hnew.at[k], move_send.at[k])

        @pl.when(final)
        def _():
            lax.fori_loop(
                0, spread, lambda b, unused: (sent(hnew.at[k, 0], fin_send, my_chunk, b), unused)[1], 0
            )

    @pl.when(starts)
    def _():
        rows_to(nx, way * last, drain_rows)

    for f in range(FLOWS):
        arrived(fin.at[f], fin_recv.at[f])
        out[f // 2, f % 2] = fin[f][:, :chunk]


def on_device(entering, norm_gain, w_gate, w_up, w_down, route_ids, route_scores):
    sections = lax.axis_size("section")
    spread = lax.axis_size("expert")
    tokens, width = entering.shape[2:]
    chunk = width // sections
    hid = w_gate.shape[2]
    nx = sections // NZ
    topk = route_ids.shape[4]
    window = spread // GROUP
    rows = spread * CAP
    slots = spread // 2 * CAP * window
    count = spread // 2 * tokens
    lanes = FLOWS * 2 * window * CAP
    vmem = pl.BlockSpec(memory_space=pltpu.VMEM)
    hbm = pl.BlockSpec(memory_space=pl.ANY)
    dma = pltpu.SemaphoreType.DMA
    return pl.pallas_call(
        kernel,
        out_shape=jax.ShapeDtypeStruct((2, 2, tokens, chunk), BF16),
        in_specs=[hbm, hbm, hbm, hbm, hbm, hbm, hbm],
        out_specs=vmem,
        scratch_shapes=[
            pltpu.VMEM((width, hid), BF16),
            pltpu.VMEM((width, hid), BF16),
            pltpu.VMEM((hid, width), BF16),
            pltpu.VMEM((2, 2, tokens, chunk * NY), BF16),
            pltpu.VMEM((2, NY, tokens, WIDE), BF16),
            pltpu.VMEM((sections, WIDE), F32),
            pltpu.VMEM((FLOWS, sections, rows, WIDE), BF16),
            pltpu.VMEM((FLOWS, nx, NY // 2, rows, WIDE), BF16),
            pltpu.VMEM((nx, rows, chunk * NY), BF16),
            pltpu.VMEM((rows, hid), BF16),
            pltpu.VMEM((nx, spread, tokens, WIDE), BF16),
            pltpu.VMEM((nx, spread, tokens, WIDE), BF16),
            pltpu.VMEM((nx + 1, window, rows, WIDE), BF16),
            pltpu.VMEM((nx, window, rows, WIDE), BF16),
            pltpu.VMEM((FLOWS, tokens, WIDE), BF16),
            pltpu.VMEM((1, 1, lanes), F32),
            pltpu.VMEM((2 * nx + 1, spread, 1, lanes), F32),
            pltpu.VMEM((2, count, slots), BF16),
            pltpu.VMEM((2, count, slots), BF16),
            pltpu.VMEM((2, slots, count), BF16),
            pltpu.VMEM((2, slots, WIDE), F32),
            pltpu.VMEM((2, slots, slots), BF16),
            pltpu.VMEM((2, slots, slots), BF16),
            pltpu.VMEM((1, width), F32),
            pltpu.VMEM((2, 2, 1, topk, tokens), jnp.int32),
            pltpu.VMEM((2, 2, 1, topk, tokens), F32),
            dma((3,)),
            pltpu.VMEM((FLOWS, nx, NY // 2, rows, WIDE), BF16),
            pltpu.VMEM((FLOWS, nx, NY // 2, rows, WIDE), BF16),
            dma((FLOWS,)),
            dma((FLOWS, sections)),
            dma((FLOWS,)),
            dma((3,)),
            dma,
            dma((2, NY)),
            dma,
            dma((FLOWS, sections)),
            dma((FLOWS,)),
            dma((nx + 1,)),
            dma((nx,)),
            dma((nx,)),
            dma((nx,)),
            dma,
            dma((FLOWS,)),
            dma,
            dma((2 * nx + 1,)),
        ],
        compiler_params=pltpu.CompilerParams(
            has_side_effects=True, vmem_limit_bytes=60 * 2**20
        ),
        cost_estimate=pl.CostEstimate(
            flops=2 * FLOWS * rows * width * hid * 3,
            bytes_accessed=width * hid * 6,
            transcendentals=0,
        ),
        name="relay",
    )(
        entering, norm_gain, w_gate, w_up, w_down,
        jnp.swapaxes(route_ids, 3, 4), jnp.swapaxes(route_scores, 3, 4),
    )


def solution(mesh):
    return jax.shard_map(
        on_device,
        mesh=mesh,
        in_specs=(
            P(None, None, "expert", None),
            P("section", None),
            P("section", None, "expert"),
            P("section", None, "expert"),
            P("section", "expert", None),
            P(None, None, "section", "expert", None),
            P(None, None, "section", "expert", None),
        ),
        out_specs=P(None, None, "expert", "section"),
        check_vma=False,
    )
```
